128 devices in a mesh: cp: 8 (over x, core), dp: 16 (over y, z).
Axes of the slice: x: 4, y: 4, z: 4, core: 2. Of those that a mesh axis runs over, the one named last changes fastest.
Arguments:
- q_nope: bfloat16 [2, 16, 1024, 32, 128], P(None, 'dp', 'cp'), may hold values from -3 to 3
- q_rope: bfloat16 [2, 16, 1024, 2048], P(None, 'dp', 'cp'), may hold values from -310 to 310, as said below
- grad_out: bfloat16 [2, 16, 1024, 32, 128], P(None, 'dp', 'cp'), may hold values from -6 to 6
- latent: bfloat16 [16, 1024, 512], P('dp', 'cp'), may hold values from -6 to 6
- key_rope: bfloat16 [16, 64, 1024], P('dp', None, 'cp'), may hold values from -6 to 6
- hidden_in: bfloat16 [16, 1024, 7168], P('dp', 'cp'), may hold values from -6 to 6
- w_uk: bfloat16 [2, 32, 128, 512], replicated, may hold values from -0.5 to 0.5
- w_uv: bfloat16 [2, 32, 512, 128], replicated, may hold values from -0.25 to 0.25
- doc_lengths: int32 [16, 32], P('dp'), may hold values from 1 to 192, 1024 in all within a row
- plan: int32 [16, 8, 8], P('dp'), may hold values from 0 to 7, each once within a row
Outputs:
- dq_nope: bfloat16 [2, 16, 1024, 32, 128], P(None, 'dp', 'cp')
- dq_rope: bfloat16 [2, 16, 1024, 2048], P(None, 'dp', 'cp')
- d_latent: bfloat16 [16, 1024, 512], P('dp', 'cp')
- d_key_rope: bfloat16 [16, 64, 1024], P('dp', None, 'cp')
- d_wdkv: float32 [7168, 576], P(('cp', 'dp'))
The draws below stay inside these ranges and needn't reach their ends.
Inputs may be any that keep to these rules, and one draw needn't show every extreme that they name: `q_rope`: in the hidden draw some queries point strongly at nearby keys. `doc_lengths`: each packed batch holds 32 documents that fill its 1024 tokens; the longest has exactly 192 tokens. Each row plan[p, d] is a permutation of 0 to 7.
All inputs are finite; a program needn't handle non-finite values.
Results may differ from the reference program's by a relative error of at most 0.009.
Values may be sent and summed in bfloat16 or wider, within the bound.
A program may use at most 192 MiB of HBM per device.

```python
import math
import jax
import jax.numpy as jnp
import numpy as np
from jax import lax

H = 32
HEAD = 128
ROPE = 64
D_LAT = 512
DM = 7168
LAYERS = 2
MAXDOC = 192
TOK_DEV = 128
TOKENS = 1024
PACKS = 16
NDOC = 32
SUB = 16
N_CP = 8


def rope_base(key):
    return jnp.clip(jax.random.normal(key, (PACKS, TOKENS, ROPE), jnp.float32), -5.0, 5.0)


def draw_key_rope(key, part):
    base = rope_base(key)
    return jnp.swapaxes(base, 1, 2).astype(jnp.bfloat16)


def draw_q_rope(key, part):
    key = jax.random.fold_in(key, 7)
    first = jax.random.fold_in(key, 0)
    drawn = jnp.clip(jax.random.normal(first, (LAYERS, PACKS, TOKENS, H, ROPE), jnp.float32), -5.0, 5.0)
    return drawn.reshape(LAYERS, PACKS, TOKENS, H * ROPE).astype(jnp.bfloat16)


def steps_of(rng, dims, shards, smallest, largest):
    def one(axis_at, shards_of):
        steps = jax.random.uniform(jax.random.fold_in(jax.random.fold_in(rng, 6), axis_at), (shards_of,), jnp.float32, smallest / len(shards), largest / len(shards))
        return jnp.repeat(jnp.exp(steps), dims[axis_at] // shards_of).reshape((-1,) + (1,) * (len(dims) - axis_at - 1))

    gain = one(*shards[0])
    for cut in shards[1:]:
        gain = gain * one(*cut)
    return gain


def length_profile(number_of, total, reach, skew):
    portions = [(1 << 20) // math.isqrt(grade ** skew) + 1 for grade in range(2, number_of + 1)]
    rest, holding = total - reach - (number_of - 1), [1] * (number_of - 1)
    while rest > 0:
        movable = [i for i in range(number_of - 1) if holding[i] < reach]
        whole, left = sum([portions[i] for i in movable]), rest
        for i in movable:
            more = min(reach - holding[i], max(1, left * portions[i] // whole), rest)
            holding[i] = holding[i] + more
            rest = rest - more
    return np.array([reach] + holding)


def uneven_parts(own_key, number_of, total, most, slope):
    if number_of == 2:
        one = jax.random.randint(own_key, (), max(1, total - most), min(most, total - 1) + 1)
        return jnp.stack([one, total - one])
    sizes = jnp.asarray(length_profile(number_of, total, most, slope), jnp.int32)
    twos = (number_of - 1) // 2
    donor, taker = sizes[1:1 + 2 * twos:2], sizes[2:2 + 2 * twos:2]
    room = jnp.minimum(donor - 1, most - taker)
    moved = jax.random.randint(jax.random.fold_in(own_key, 1), (twos,), 0, 1 << 20) % (room + 1)
    sizes = sizes.at[1:1 + 2 * twos:2].set(donor - moved).at[2:2 + 2 * twos:2].set(taker + moved)
    return sizes[jax.random.permutation(jax.random.fold_in(own_key, 2), number_of)]


def gaussian(rng, shape, spread, bound, cuts=(), held_as=jnp.bfloat16):
    loudness = steps_of(rng, shape, cuts, -0.22, 0.18) if cuts else 1.0
    values = jax.random.normal(rng, shape, jnp.float32) * spread * loudness
    return jnp.minimum(jnp.maximum(values, -bound), bound).astype(held_as)


def setup_inputs(seed: int = 0) -> dict:
    streams_of = jax.random.split(jax.random.key(seed), 11)
    return {
        "q_nope": gaussian(streams_of[0], (LAYERS, PACKS, TOKENS, H, HEAD), 0.5, 3.0, ((1, 16), (2, 8))),
        "q_rope": draw_q_rope(jax.random.fold_in(streams_of[10], 71), 0),
        "grad_out": gaussian(streams_of[2], (LAYERS, PACKS, TOKENS, H, HEAD), 1.0, 6.0, ((1, 16), (2, 8))),
        "latent": gaussian(streams_of[3], (PACKS, TOKENS, D_LAT), 1.0, 6.0, ((0, 16), (1, 8))),
        "key_rope": draw_key_rope(jax.random.fold_in(streams_of[10], 71), 0),
        "hidden_in": gaussian(streams_of[5], (PACKS, TOKENS, DM), 1.0, 6.0, ((0, 16), (1, 8))),
        "w_uk": gaussian(streams_of[6], (LAYERS, H, HEAD, D_LAT), HEAD ** -0.5, 0.5),
        "w_uv": gaussian(streams_of[7], (LAYERS, H, D_LAT, HEAD), D_LAT ** -0.5, 0.25),
        "doc_lengths": jax.vmap(lambda own: uneven_parts(own, NDOC, TOKENS, MAXDOC, 0))(jax.random.split(streams_of[8], PACKS)).reshape((PACKS, NDOC)).astype(jnp.int32),
        "plan": jax.vmap(lambda own: jax.random.permutation(own, N_CP))(jax.random.split(streams_of[9], PACKS * N_CP)).reshape((PACKS, N_CP, N_CP)).astype(jnp.int32),
    }


def doc_numbers(lengths, count):
    ends = jnp.cumsum(lengths).astype(jnp.int32)
    places = jnp.arange(count, dtype=jnp.int32)
    return lax.optimization_barrier(jnp.sum((places[:, None] >= ends[None, :]).astype(jnp.int32), axis=1))

def layer_grads(q_part, r_part, g_part, lat, rope_keys, allowed, w_key, w_val):
    ntok = lat.shape[0]
    heads = q_part.shape[1]
    f32 = jnp.float32
    scale = 1.0 / math.sqrt(HEAD + ROPE)
    q_lat = jnp.einsum('thd,hdl->thl', q_part.astype(f32), w_key.astype(f32)).astype(jnp.bfloat16)
    q_rot = r_part.reshape(ntok, heads, ROPE)
    score = jnp.einsum('thl,kl->htk', q_lat.astype(f32), lat.astype(f32))
    score = (score + jnp.einsum('thr,rk->htk', q_rot.astype(f32), rope_keys.astype(f32))) * scale
    score = jnp.where(allowed[None], score, -jnp.inf)
    top = lax.optimization_barrier(jnp.max(score, axis=2, keepdims=True))
    expd = jnp.exp(score - top)
    prob = expd / lax.optimization_barrier(jnp.sum(expd, axis=2, keepdims=True))
    g_lat = jnp.einsum('thd,hld->thl', g_part.astype(f32), w_val.astype(f32)).astype(jnp.bfloat16)
    dprob = jnp.einsum('thl,kl->htk', g_lat.astype(f32), lat.astype(f32))
    delta = lax.optimization_barrier(jnp.sum(prob * dprob, axis=2, keepdims=True))
    dscore = (prob * (dprob - delta) * scale).astype(jnp.bfloat16)
    prob_low = prob.astype(jnp.bfloat16)
    dq_lat = jnp.einsum('htk,kl->thl', dscore.astype(f32), lat.astype(f32)).astype(jnp.bfloat16)
    gq_nope = jnp.einsum('thl,hdl->thd', dq_lat.astype(f32), w_key.astype(f32)).astype(jnp.bfloat16)
    gq_rope = jnp.einsum('htk,rk->thr', dscore.astype(f32), rope_keys.astype(f32)).astype(jnp.bfloat16)
    lat_sum = jnp.einsum('htk,thl->kl', dscore.astype(f32), q_lat.astype(f32))
    lat_sum = lat_sum + jnp.einsum('htk,thl->kl', prob_low.astype(f32), g_lat.astype(f32))
    rope_sum = jnp.einsum('htk,thr->rk', dscore.astype(f32), q_rot.astype(f32))
    return (gq_nope, gq_rope.reshape(ntok, heads * ROPE), lat_sum, rope_sum)

def reference(q_nope, q_rope, grad_out, latent, key_rope, hidden_in, w_uk, w_uv, doc_lengths, plan):

    def one_pack(items):
        qn, qr, go, lat, rope_keys, lengths, table = items
        ntok = lat.shape[0]
        docs = doc_numbers(lengths, ntok)
        places = jnp.arange(ntok, dtype=jnp.int32)
        allowed = (docs[:, None] == docs[None, :]) & (places[None, :] <= places[:, None])
        nope_list = []
        rope_list = []
        lat_total = jnp.zeros(lat.shape, jnp.float32)
        rope_total = jnp.zeros(rope_keys.shape, jnp.float32)
        for layer in range(LAYERS):
            a, b, c, d = layer_grads(qn[layer], qr[layer], go[layer], lat, rope_keys, allowed, w_uk[layer], w_uv[layer])
            nope_list.append(a)
            rope_list.append(b)
            lat_total = lat_total + c
            rope_total = rope_total + d
        source = (jnp.arange(N_CP, dtype=jnp.int32)[None, :, None] * TOK_DEV + table.T.astype(jnp.int32)[:, :, None] * SUB + jnp.arange(SUB, dtype=jnp.int32)[None, None, :]).reshape(-1)
        gq_nope = jnp.take(jnp.stack(nope_list), source, axis=1)
        gq_rope = jnp.take(jnp.stack(rope_list), source, axis=1)
        return (gq_nope, gq_rope, lat_total.astype(jnp.bfloat16), rope_total.astype(jnp.bfloat16))
    dq_nope, dq_rope, d_latent, d_key_rope = lax.map(one_pack, (jnp.moveaxis(q_nope, 1, 0), jnp.moveaxis(q_rope, 1, 0), jnp.moveaxis(grad_out, 1, 0), latent, key_rope, doc_lengths, plan))
    dq_nope = jnp.moveaxis(dq_nope, 0, 1)
    dq_rope = jnp.moveaxis(dq_rope, 0, 1)
    joined = jnp.concatenate([d_latent, jnp.swapaxes(d_key_rope, 1, 2)], axis=2)
    d_wdkv = jnp.einsum('ptm,ptc->mc', hidden_in.astype(jnp.float32), joined.astype(jnp.float32))
    return (dq_nope, dq_rope, d_latent, d_key_rope, d_wdkv)
```

```python
import functools
import math

import jax
import jax.numpy as jnp
from jax import lax
from jax.experimental import pallas as pl
from jax.experimental.pallas import tpu as pltpu
from jax.sharding import PartitionSpec as P

BF = jnp.bfloat16
F32 = jnp.float32
MARGIN = 192
SUB = 64
WIN = 256
HG = 8


def dot(a, b, ca, cb):
    return lax.dot_general(a, b, (((ca,), (cb,)), ((), ())), preferred_element_type=F32)


def attention(
    lens, order, qn_h, qr_h, go_h, le_h, wk_h, wv_h,
    on, orp, acc,
    qn, qr, go, le, wk, wv, qf, gf, of, ro, ql, gl, dq, bias, sem_q, sem_w,
):
    layers, rows, head = qn.shape
    tok = qr.shape[1]
    heads = rows // tok
    lat = gl.shape[2]
    steps = heads // HG
    blk = tok // on.shape[0]
    scale = 1.0 / math.sqrt(head + 64)
    me = lax.axis_index("cp")

    def q_copies(layer):
        return [
            pltpu.make_async_copy(qn_h.at[layer], qn.at[layer], sem_q.at[layer, 0]),
            pltpu.make_async_copy(go_h.at[layer], go.at[layer], sem_q.at[layer, 1]),
            pltpu.make_async_copy(qr_h.at[layer], qr.at[layer], sem_q.at[layer, 2]),
        ]

    def w_copies(layer, step):
        part = pl.ds(step * HG, HG)
        return [
            pltpu.make_async_copy(wk_h.at[layer, part], wk.at[layer, part], sem_w.at[layer, step, 0]),
            pltpu.make_async_copy(wv_h.at[layer, part], wv.at[layer, part], sem_w.at[layer, step, 1]),
        ]

    keys = pltpu.make_async_copy(le_h, le, sem_q.at[layers, 0])
    keys.start()
    for layer in range(layers):
        for c in q_copies(layer):
            c.start()
        for step in range(steps):
            for c in w_copies(layer, step):
                c.start()

    acc[...] = jnp.zeros_like(acc)
    for s in range(2):
        t = me * tok + s * SUB + lax.broadcasted_iota(jnp.int32, (SUB, 128), 0)
        first = jnp.zeros((SUB, 128), jnp.int32)
        end = jnp.int32(0)
        for j in range(lens.shape[0]):
            end = end + lens[j]
            first = jnp.where(end <= t, end, first)
        for half in range(2):
            u = (
                me * tok - MARGIN + s * SUB + half * 128
                + lax.broadcasted_iota(jnp.int32, (SUB, 128), 1)
            )
            ok = (u >= first) & (u <= t)
            bias[s, :, half * 128 : half * 128 + 128] = jnp.where(ok, jnp.inf, -jnp.inf)
    keys.wait()
    low = lax.broadcasted_iota(jnp.int32, (SUB, 128), 1) < 64

    def layer_body(layer, carry):
        for c in q_copies(layer):
            c.wait()

        def widen(c, carry):
            part = pl.ds(pl.multiple_of(c * 512, 512), 512)
            qf[part, :] = qn[layer, part, :].astype(F32)
            gf[part, :] = go[layer, part, :].astype(F32)
            return carry

        lax.fori_loop(0, rows // 512, widen, 0)

        def step_body(step, carry):
            for c in w_copies(layer, step):
                c.wait()
            base = step * HG
            for i in range(HG):
                h = base + i
                qh = qf[pl.ds(h, tok, stride=heads), :].astype(BF)
                gh = gf[pl.ds(h, tok, stride=heads), :].astype(BF)
                a = dot(qh, wk[layer, h], 1, 0).astype(BF)
                b = dot(gh, wv[layer, h], 1, 1).astype(BF)
                lanes = pl.ds(pl.multiple_of((step * (HG // 2) + i // 2) * 128, 128), 128)
                for s in range(2):
                    mine = slice(i * SUB, i * SUB + SUB)
                    ql[s, mine, :lat] = a[s * SUB : s * SUB + SUB]
                    gl[s, mine, :] = b[s * SUB : s * SUB + SUB]
                    pair = qr[layer, s * SUB : s * SUB + SUB, lanes].astype(F32)
                    pair = jnp.where(low if i % 2 == 0 else ~low, pair, 0.0)
                    ql[s, mine, lat:] = pair.astype(BF)
            for s in range(2):
                win = slice(s * SUB, s * SUB + WIN)
                score = dot(ql[s], le[win, :], 1, 1) * scale
                score = jnp.minimum(score.reshape(HG, SUB, WIN), bias[s][None])
                score = score.reshape(HG * SUB, WIN)
                top = jnp.max(score, axis=1, keepdims=True)
                e = jnp.exp(score - top)
                prob = e * (1.0 / jnp.sum(e, axis=1, keepdims=True))
                dprob = dot(gl[s], le[win, :lat], 1, 1)
                delta = jnp.sum(prob * dprob, axis=1, keepdims=True)
                ds = (prob * (dprob - delta) * scale).astype(BF)
                low_p = prob.astype(BF)
                d = dot(ds, le[win, :], 1, 0)
                for i in range(HG):
                    dq[i, s * SUB : s * SUB + SUB, :] = d[i * SUB : i * SUB + SUB, :lat].astype(BF)
                for j in range(HG // 2):
                    even = d[2 * j * SUB : (2 * j + 1) * SUB, lat:]
                    odd = d[(2 * j + 1) * SUB : (2 * j + 2) * SUB, lat:]
                    lanes = pl.ds(pl.multiple_of((step * (HG // 2) + j) * 128, 128), 128)
                    ro[s * SUB : s * SUB + SUB, lanes] = jnp.where(low, even, odd).astype(BF)
                acc[win, :] += dot(ds, ql[s], 0, 0)
                acc[win, :lat] += dot(low_p, gl[s], 0, 0)
            for i in range(HG):
                h = base + i
                of[pl.ds(h, tok, stride=heads), :] = dot(dq[i], wk[layer, h], 1, 1)
            return carry

        lax.fori_loop(0, steps, step_body, 0)

        def place(k, carry):
            b = order[k]
            on[k, layer] = of[pl.ds(pl.multiple_of(b * (blk * heads), blk * heads), blk * heads), :].astype(BF)
            orp[k, layer] = ro[pl.ds(pl.multiple_of(b * blk, blk), blk), :]
            return carry

        lax.fori_loop(0, on.shape[0], place, 0)
        return carry

    lax.fori_loop(0, layers, layer_body, 0)


def call_attention(lens, order, qn, qr, go, le, wk, wv, groups):
    layers, rows, head = qn.shape
    tok, wide = qr.shape[1:]
    heads = rows // tok
    span, ext = le.shape
    lat = wk.shape[3]
    smem = pl.BlockSpec(memory_space=pltpu.SMEM)
    hbm = pl.BlockSpec(memory_space=pl.ANY)
    vmem = pl.BlockSpec(memory_space=pltpu.VMEM)
    return pl.pallas_call(
        attention,
        out_shape=(
            jax.ShapeDtypeStruct((groups, layers, rows // groups, head), BF),
            jax.ShapeDtypeStruct((groups, layers, tok // groups, wide), BF),
            jax.ShapeDtypeStruct((span, ext), F32),
        ),
        in_specs=[smem, smem] + [hbm] * 6,
        out_specs=(vmem, vmem, vmem),
        scratch_shapes=[
            pltpu.VMEM(qn.shape, BF),
            pltpu.VMEM(qr.shape, BF),
            pltpu.VMEM(go.shape, BF),
            pltpu.VMEM(le.shape, BF),
            pltpu.VMEM(wk.shape, BF),
            pltpu.VMEM(wv.shape, BF),
            pltpu.VMEM((rows, head), F32),
            pltpu.VMEM((rows, head), F32),
            pltpu.VMEM((rows, head), F32),
            pltpu.VMEM((tok, wide), BF),
            pltpu.VMEM((2, HG * SUB, ext), BF),
            pltpu.VMEM((2, HG * SUB, lat), BF),
            pltpu.VMEM((HG, tok, lat), BF),
            pltpu.VMEM((2, SUB, WIN), F32),
            pltpu.SemaphoreType.DMA((layers + 1, 3)),
            pltpu.SemaphoreType.DMA((layers, heads // HG, 2)),
        ],
        compiler_params=pltpu.CompilerParams(vmem_limit_bytes=60 * 1024 * 1024),
    )(lens, order, qn, qr, go, le, wk, wv)


def shift(value, by):
    n = lax.axis_size("cp")
    return lax.ppermute(value, "cp", [(i, (i + by) % n) for i in range(n)])


def on_device(q_nope, q_rope, grad_out, latent, key_rope, hidden_in, w_uk, w_uv, doc_lengths, plan):
    groups = lax.axis_size("cp")
    me = lax.axis_index("cp")
    layers, _, tok, heads, head = q_nope.shape
    lat = latent.shape[2]
    turned = key_rope[0].T
    own = jnp.concatenate([latent[0], turned, turned], axis=1)
    le = jnp.concatenate([shift(own[2 * tok - MARGIN :], 2), shift(own, 1), own], axis=0)
    on, orp, acc = call_attention(
        doc_lengths[0],
        plan[0][me],
        q_nope.reshape(layers, tok * heads, head),
        q_rope[:, 0],
        grad_out.reshape(layers, tok * heads, head),
        le,
        w_uk,
        w_uv,
        groups,
    )
    on = lax.all_to_all(on, "cp", split_axis=0, concat_axis=0, tiled=True)
    orp = lax.all_to_all(orp, "cp", split_axis=0, concat_axis=0, tiled=True)
    dq_nope = jnp.swapaxes(on, 0, 1).reshape(layers, 1, tok, heads, head)
    dq_rope = jnp.swapaxes(orp, 0, 1).reshape(q_rope.shape)
    part = jnp.concatenate([acc[:, :lat], acc[:, lat : lat + 64] + acc[:, lat + 64 :]], axis=1)
    edge = MARGIN - tok
    total = part[MARGIN:] + shift(part[edge:MARGIN], -1)
    total = total.at[tok - edge :].add(shift(part[:edge], -2))
    joined = total.astype(BF)
    d_latent = joined[:, :lat]
    rope_low = joined[:, lat:]
    cols = lax.all_to_all(hidden_in[0], "cp", split_axis=1, concat_axis=0, tiled=True)
    keys = lax.all_gather(joined, "cp", axis=0, tiled=True)
    d_wdkv = lax.psum_scatter(dot(cols, keys, 0, 0), "dp", scatter_dimension=0, tiled=True)
    return dq_nope, dq_rope, d_latent[None], rope_low.T[None], d_wdkv


def solution(mesh):
    placed = (
        P(None, "dp", "cp", None, None),
        P(None, "dp", "cp", None),
        P(None, "dp", "cp", None, None),
        P("dp", "cp", None),
        P("dp", None, "cp"),
        P("dp", "cp", None),
        P(),
        P(),
        P("dp", None),
        P("dp", None, None),
    )
    return jax.shard_map(
        on_device,
        mesh=mesh,
        in_specs=placed,
        out_specs=(
            P(None, "dp", "cp", None, None),
            P(None, "dp", "cp", None),
            P("dp", "cp", None),
            P("dp", None, "cp"),
            P(("cp", "dp"), None),
        ),
        check_vma=False,
    )
```

```python
import functools
import math

import jax
import jax.numpy as jnp
from jax import lax
from jax.experimental import pallas as pl
from jax.experimental.pallas import tpu as pltpu
from jax.sharding import PartitionSpec as P

BF = jnp.bfloat16
F32 = jnp.float32
MESH = pl.DeviceIdType.MESH
MARGIN = 192
SUB = 64
WIN = 256
HG = 8
ROPE = 64
PIECE = 64


def dot(a, b, ca, cb):
    return lax.dot_general(a, b, (((ca,), (cb,)), ((), ())), preferred_element_type=F32)


def each(count, body):
    def step(i, carry):
        body(i)
        return carry

    lax.fori_loop(0, count, step, 0)


def kernel(
    ncp, ndp, side,
    lens, plan, qn_h, qr_h, go_h, lat_h, kr_h, hid_h, wk_h, wv_h,
    dqn_h, dqr_h, dlat, dkr, dw,
    qn, qr, go, le, kr, hid, wk, wv, qf, gf, of, ro, ql, gl, dq, bias, acc, on, orp,
    slab, ht, hr, back, back1, back2, joined, jr, part, parts,
    sem_q, sem_w, sem_k, sem_halo, sem_hs, sem_hr, sem_os, sem_or, sem_back,
    sem_near, sem_fwd_s, sem_fwd_r, sem_ps, sem_pr, sem_own,
):
    layers, rows, head = qn.shape
    tok = qr.shape[1]
    heads = rows // tok
    lat = gl.shape[2]
    ext = le.shape[1]
    steps = heads // HG
    blk = tok // ncp
    scale = 1.0 / math.sqrt(head + ROPE)
    c_me = lax.axis_index("cp")
    d_me = lax.axis_index("dp")

    def cp_dev(offset):
        return lax.rem(c_me + offset + ncp, ncp)

    def dp_dev(offset):
        return lax.rem(d_me + offset + ndp, ndp)

    def q_copies(layer):
        return [
            pltpu.make_async_copy(qn_h.at[layer], qn.at[layer], sem_q.at[layer, 0]),
            pltpu.make_async_copy(go_h.at[layer], go.at[layer], sem_q.at[layer, 1]),
            pltpu.make_async_copy(qr_h.at[layer], qr.at[layer], sem_q.at[layer, 2]),
        ]

    def w_copies(layer, step):
        heads_of = pl.ds(step * HG, HG)
        return [
            pltpu.make_async_copy(wk_h.at[layer, heads_of], wk.at[layer, heads_of], sem_w.at[layer, step, 0]),
            pltpu.make_async_copy(wv_h.at[layer, heads_of], wv.at[layer, heads_of], sem_w.at[layer, step, 1]),
        ]

    own_rows = slice(MARGIN, MARGIN + tok)
    edge = MARGIN - tok
    k_copies = [
        pltpu.make_async_copy(lat_h, le.at[own_rows, :lat], sem_k.at[0]),
        pltpu.make_async_copy(kr_h, kr, sem_k.at[1]),
        pltpu.make_async_copy(hid_h, hid, sem_k.at[2]),
    ]
    for c in k_copies:
        c.start()
    for layer in range(layers):
        for c in q_copies(layer):
            c.start()
        for step in range(steps):
            for c in w_copies(layer, step):
                c.start()

    barrier = pltpu.get_barrier_semaphore()

    def greet_cp(i):
        pl.semaphore_signal(barrier, inc=1, device_id=(cp_dev(i + 1), d_me), device_id_type=MESH)

    def greet_dp(i):
        pl.semaphore_signal(barrier, inc=1, device_id=(c_me, dp_dev(i + 1)), device_id_type=MESH)

    each(ncp - 1, greet_cp)
    each(ndp - 1, greet_dp)

    k_copies[0].wait()
    k_copies[1].wait()
    turned = kr[...].astype(F32)
    le[own_rows, lat:] = jnp.concatenate([turned, turned], axis=0).T.astype(BF)
    pl.semaphore_wait(barrier, ncp + ndp - 2)

    halo = [
        pltpu.make_async_remote_copy(
            le.at[own_rows], le.at[edge:MARGIN], sem_halo.at[0], sem_halo.at[1],
            device_id=(cp_dev(1), d_me), device_id_type=MESH,
        ),
        pltpu.make_async_remote_copy(
            le.at[MARGIN + tok - edge : MARGIN + tok], le.at[:edge], sem_halo.at[2], sem_halo.at[3],
            device_id=(cp_dev(2), d_me), device_id_type=MESH,
        ),
    ]
    for c in halo:
        c.start()

    k_copies[2].wait()
    width = hid.shape[1] // ncp
    rows_dev = width // ndp

    def turn(c):
        for j in range(width // 128):
            lanes = pl.ds(pl.multiple_of(c * width + j * 128, 128), 128)
            slab[j * 128 : j * 128 + 128, :] = hid[:, lanes].astype(F32).T
        pad = jnp.zeros((PIECE - rows_dev, tok), F32)
        for j in range(ndp):
            piece = jnp.concatenate([slab[j * rows_dev : (j + 1) * rows_dev, :], pad], axis=0)
            ht[j, pl.ds(pl.multiple_of(c * PIECE, PIECE), PIECE), :] = piece.astype(BF)

    each(ncp, turn)

    def my_lanes():
        return pl.ds(pl.multiple_of(d_me * tok, tok), tok)

    def hidden_copy(i):
        to = dp_dev(i + 1)
        return pltpu.make_async_remote_copy(
            ht.at[to], hr.at[:, my_lanes()], sem_hs.at[i], sem_hr.at[i],
            device_id=(c_me, to), device_id_type=MESH,
        )

    each(ndp - 1, lambda i: hidden_copy(i).start())
    hidden_own = pltpu.make_async_copy(ht.at[d_me], hr.at[:, my_lanes()], sem_own.at[0])
    hidden_own.start()

    acc[...] = jnp.zeros_like(acc)
    for s in range(2):
        t = c_me * tok + s * SUB + lax.broadcasted_iota(jnp.int32, (SUB, 128), 0)
        first = jnp.zeros((SUB, 128), jnp.int32)
        end = jnp.int32(0)
        for j in range(lens.shape[1]):
            end = end + lens[0, j]
            first = jnp.where(end <= t, end, first)
        for half in range(2):
            u = (
                c_me * tok - MARGIN + s * SUB + half * 128
                + lax.broadcasted_iota(jnp.int32, (SUB, 128), 1)
            )
            ok = (u >= first) & (u <= t)
            bias[s, :, half * 128 : half * 128 + 128] = jnp.where(ok, jnp.inf, -jnp.inf)
    low = lax.broadcasted_iota(jnp.int32, (SUB, 128), 1) < ROPE
    for c in halo:
        c.wait_recv()

    def out_copies(layer, i):
        to = cp_dev(i + 1)
        return [
            pltpu.make_async_remote_copy(
                on.at[to, layer],
                dqn_h.at[layer, pl.ds(pl.multiple_of(c_me * (blk * heads), blk * heads), blk * heads)],
                sem_os.at[layer, i, 0], sem_or.at[layer, i, 0],
                device_id=(to, d_me), device_id_type=MESH,
            ),
            pltpu.make_async_remote_copy(
                orp.at[to, layer],
                dqr_h.at[layer, pl.ds(pl.multiple_of(c_me * blk, blk), blk)],
                sem_os.at[layer, i, 1], sem_or.at[layer, i, 1],
                device_id=(to, d_me), device_id_type=MESH,
            ),
        ]

    def out_own(layer):
        return [
            pltpu.make_async_copy(
                on.at[c_me, layer],
                dqn_h.at[layer, pl.ds(pl.multiple_of(c_me * (blk * heads), blk * heads), blk * heads)],
                sem_own.at[1 + 2 * layer],
            ),
            pltpu.make_async_copy(
                orp.at[c_me, layer],
                dqr_h.at[layer, pl.ds(pl.multiple_of(c_me * blk, blk), blk)],
                sem_own.at[2 + 2 * layer],
            ),
        ]

    def compute(layer):
        for c in q_copies(layer):
            c.wait()

        def widen(c):
            chunk = pl.ds(pl.multiple_of(c * 512, 512), 512)
            qf[chunk, :] = qn[layer, chunk, :].astype(F32)
            gf[chunk, :] = go[layer, chunk, :].astype(F32)

        each(rows // 512, widen)

        def step_body(step):
            for c in w_copies(layer, step):
                c.wait()
            base = step * HG
            for i in range(HG):
                h = base + i
                qh = qf[pl.ds(h, tok, stride=heads), :].astype(BF)
                gh = gf[pl.ds(h, tok, stride=heads), :].astype(BF)
                a = dot(qh, wk[layer, h], 1, 0).astype(BF)
                b = dot(gh, wv[layer, h], 1, 1).astype(BF)
                lanes = pl.ds(pl.multiple_of((step * (HG // 2) + i // 2) * 128, 128), 128)
                for s in range(2):
                    mine = slice(i * SUB, i * SUB + SUB)
                    ql[s, mine, :lat] = a[s * SUB : s * SUB + SUB]
                    gl[s, mine, :] = b[s * SUB : s * SUB + SUB]
                    pair = qr[layer, s * SUB : s * SUB + SUB, lanes].astype(F32)
                    pair = jnp.where(low if i % 2 == 0 else ~low, pair, 0.0)
                    ql[s, mine, lat:] = pair.astype(BF)
            for s in range(2):
                win = slice(s * SUB, s * SUB + WIN)
                score = dot(ql[s], le[win, :], 1, 1) * scale
                score = jnp.minimum(score.reshape(HG, SUB, WIN), bias[s][None])
                score = score.reshape(HG * SUB, WIN)
                top = jnp.max(score, axis=1, keepdims=True)
                e = jnp.exp(score - top)
                prob = e * (1.0 / jnp.sum(e, axis=1, keepdims=True))
                dprob = dot(gl[s], le[win, :lat], 1, 1)
                delta = jnp.sum(prob * dprob, axis=1, keepdims=True)
                ds = (prob * (dprob - delta) * scale).astype(BF)
                low_p = prob.astype(BF)
                d = dot(ds, le[win, :], 1, 0)
                for i in range(HG):
                    dq[i, s * SUB : s * SUB + SUB, :] = d[i * SUB : i * SUB + SUB, :lat].astype(BF)
                for j in range(HG // 2):
                    even = d[2 * j * SUB : (2 * j + 1) * SUB, lat:]
                    odd = d[(2 * j + 1) * SUB : (2 * j + 2) * SUB, lat:]
                    lanes = pl.ds(pl.multiple_of((step * (HG // 2) + j) * 128, 128), 128)
                    both = jnp.where(low, even, odd).astype(BF)
                    for q in range(SUB // blk):
                        ro[s * (SUB // blk) + q, :, lanes] = both[q * blk : q * blk + blk]
                acc[win, :] += dot(ds, ql[s], 0, 0)
                acc[win, :lat] += dot(low_p, gl[s], 0, 0)
            for i in range(HG):
                h = base + i
                back_q = dot(dq[i], wk[layer, h], 1, 1)
                for q in range(ncp):
                    of[q, pl.ds(h, blk, stride=heads), :] = back_q[q * blk : q * blk + blk]

        each(steps, step_body)

    def send_out(layer):
        def place(k):
            b = plan[0, c_me, k]
            on[k, layer] = of[b].astype(BF)
            orp[k, layer] = ro[b]

        each(ncp, place)

        def start(i):
            for c in out_copies(layer, i):
                c.start()

        each(ncp - 1, start)
        for c in out_own(layer):
            c.start()

    back_copies = [
        pltpu.make_async_remote_copy(
            back.at[edge:MARGIN], back1, sem_back.at[0], sem_back.at[1],
            device_id=(cp_dev(-1), d_me), device_id_type=MESH,
        ),
        pltpu.make_async_remote_copy(
            back.at[:edge], back2, sem_back.at[2], sem_back.at[3],
            device_id=(cp_dev(-2), d_me), device_id_type=MESH,
        ),
    ]

    def run_layer(layer):
        compute(layer)

        @pl.when(layer == layers - 1)
        def _():
            back[...] = acc[:MARGIN, :].astype(BF)
            for c in back_copies:
                c.start()

        send_out(layer)

    each(layers, run_layer)

    for c in back_copies:
        c.wait_recv()
    total = acc[own_rows, :] + back1[...].astype(F32)
    late = total[tok - edge :] + back2[...].astype(F32)
    total = jnp.concatenate([total[: tok - edge], late], axis=0)
    rope = total[:, lat:]
    rope = rope + pltpu.roll(rope, ROPE, 1)
    low_all = lax.broadcasted_iota(jnp.int32, (tok, 128), 1) < ROPE
    rope = jnp.where(low_all, rope, 0.0)
    joined[:, :lat] = total[:, :lat].astype(BF)
    joined[:, lat:] = rope.astype(BF)
    dlat[...] = total[:, :lat].astype(BF)
    dkr[...] = rope.T[:ROPE].astype(BF)

    y, z = d_me // side, lax.rem(d_me, side)
    other = ndp // side
    half = tok // 2

    def place_of(yy, zz, which):
        return jr.at[pl.ds(pl.multiple_of((yy * side + zz) * tok + which * half, half), half)]

    def ring(value, offset, n):
        return lax.rem(value + offset + n, n)

    def near(which, k):
        src = joined.at[which * half : which * half + half]
        to = y * side + ring(z, k, side) if which == 0 else ring(y, k, other) * side + z
        return pltpu.make_async_remote_copy(
            src, place_of(y, z, which), sem_near.at[which, 0, k - 1], sem_near.at[which, 1, k - 1],
            device_id=(c_me, to), device_id_type=MESH,
        )

    def forward(which, j, k):
        if which == 0:
            ref = place_of(y, ring(z, -j, side), 0)
            to = ring(y, k, other) * side + z
        else:
            ref = place_of(ring(y, -j, other), z, 1)
            to = y * side + ring(z, k, side)
        src = joined.at[which * half : which * half + half] if j == 0 else ref
        return pltpu.make_async_remote_copy(
            src, ref, sem_fwd_s.at[which, j, k - 1], sem_fwd_r.at[which, j, k - 1],
            device_id=(c_me, to), device_id_type=MESH,
        )

    for k in (1, 3, 2):
        near(0, k).start()
        near(1, k).start()
    for k in (1, 3, 2):
        forward(0, 0, k).start()
        forward(1, 0, k).start()
    gather_own = pltpu.make_async_copy(
        joined, jr.at[pl.ds(pl.multiple_of(d_me * tok, tok), tok)], sem_own.at[0]
    )
    hidden_own.wait()
    gather_own.start()
    for j in (1, 3, 2):
        for which in range(2):
            near(which, j).wait_recv()
            for k in (1, 3, 2):
                forward(which, j, k).start()
    each(ndp - 1, lambda i: hidden_copy(i).wait())
    gather_own.wait()
    for j in range(4):
        for which in range(2):
            for k in (1, 2, 3):
                forward(which, j, k).wait_recv()

    def product(c):
        piece = pl.ds(pl.multiple_of(c * 128, 128), 128)
        part[piece, :] = dot(hr[piece, :], jr[...], 1, 0).astype(BF)

    each(part.shape[0] // 128, product)

    def part_copy(i):
        to = cp_dev(i + 1)
        return pltpu.make_async_remote_copy(
            part.at[pl.ds(pl.multiple_of(to * PIECE, PIECE), PIECE)], parts.at[i],
            sem_ps.at[i], sem_pr.at[i], device_id=(to, d_me), device_id_type=MESH,
        )

    each(ncp - 1, lambda i: part_copy(i).start())
    mine = part[pl.ds(pl.multiple_of(c_me * PIECE, PIECE), PIECE), :].astype(F32)
    for i in range(ncp - 1):
        part_copy(i).wait_recv()
        mine = mine + parts[i].astype(F32)
    dw[...] = mine[:rows_dev, : lat + ROPE]

    for c in halo + back_copies:
        c.wait_send()
    for which in range(2):
        for k in (1, 2, 3):
            near(which, k).wait_send()
        for j in range(4):
            for k in (1, 2, 3):
                forward(which, j, k).wait_send()
    each(ncp - 1, lambda i: part_copy(i).wait_send())
    for layer in range(layers):
        for c in out_own(layer):
            c.wait()

        def finish(i):
            for c in out_copies(layer, i):
                c.wait()

        each(ncp - 1, finish)


def on_device(q_nope, q_rope, grad_out, latent, key_rope, hidden_in, w_uk, w_uv, doc_lengths, plan):
    ncp = lax.axis_size("cp")
    ndp = lax.axis_size("dp")
    side = math.isqrt(ndp)
    layers, _, tok, heads, head = q_nope.shape
    wide = q_rope.shape[3]
    lat = latent.shape[2]
    model = hidden_in.shape[2]
    ext = lat + 2 * ROPE
    rows = tok * heads
    smem = pl.BlockSpec(memory_space=pltpu.SMEM)
    hbm = pl.BlockSpec(memory_space=pl.ANY)
    vmem = pl.BlockSpec(memory_space=pltpu.VMEM)
    dma = pltpu.SemaphoreType.DMA
    dqn, dqr, dlat, dkr, dw = pl.pallas_call(
        functools.partial(kernel, ncp, ndp, side),
        out_shape=(
            jax.ShapeDtypeStruct((layers, rows, head), BF),
            jax.ShapeDtypeStruct((layers, tok, wide), BF),
            jax.ShapeDtypeStruct((tok, lat), BF),
            jax.ShapeDtypeStruct((ROPE, tok), BF),
            jax.ShapeDtypeStruct((model // (ncp * ndp), lat + ROPE), F32),
        ),
        in_specs=[smem, smem] + [hbm] * 8,
        out_specs=(hbm, hbm, vmem, vmem, vmem),
        scratch_shapes=[
            pltpu.VMEM((layers, rows, head), BF),
            pltpu.VMEM((layers, tok, wide), BF),
            pltpu.VMEM((layers, rows, head), BF),
            pltpu.VMEM((MARGIN + tok, ext), BF),
            pltpu.VMEM((ROPE, tok), BF),
            pltpu.VMEM((tok, model), BF),
            pltpu.VMEM(w_uk.shape, BF),
            pltpu.VMEM(w_uv.shape, BF),
            pltpu.VMEM((rows, head), F32),
            pltpu.VMEM((rows, head), F32),
            pltpu.VMEM((ncp, rows // ncp, head), F32),
            pltpu.VMEM((ncp, tok // ncp, wide), BF),
            pltpu.VMEM((2, HG * SUB, ext), BF),
            pltpu.VMEM((2, HG * SUB, lat), BF),
            pltpu.VMEM((HG, tok, lat), BF),
            pltpu.VMEM((2, SUB, WIN), F32),
            pltpu.VMEM((MARGIN + tok, ext), F32),
            pltpu.VMEM((ncp, layers, rows // ncp, head), BF),
            pltpu.VMEM((ncp, layers, tok // ncp, wide), BF),
            pltpu.VMEM((model // ncp, tok), F32),
            pltpu.VMEM((ndp, ncp * PIECE, tok), BF),
            pltpu.VMEM((ncp * PIECE, ndp * tok), BF),
            pltpu.VMEM((MARGIN, ext), BF),
            pltpu.VMEM((tok, ext), BF),
            pltpu.VMEM((MARGIN - tok, ext), BF),
            pltpu.VMEM((tok, ext), BF),
            pltpu.VMEM((ndp * tok, ext), BF),
            pltpu.VMEM((ncp * PIECE, ext), BF),
            pltpu.VMEM((ncp - 1, PIECE, ext), BF),
            dma((layers, 3)),
            dma((layers, heads // HG, 2)),
            dma((3,)),
            dma((4,)),
            dma((ndp - 1,)),
            dma((ndp - 1,)),
            dma((layers, ncp - 1, 2)),
            dma((layers, ncp - 1, 2)),
            dma((4,)),
            dma((2, 2, 3)),
            dma((2, 4, 3)),
            dma((2, 4, 3)),
            dma((ncp - 1,)),
            dma((ncp - 1,)),
            dma((1 + 2 * layers,)),
        ],
        compiler_params=pltpu.CompilerParams(
            collective_id=0, has_side_effects=True, vmem_limit_bytes=60 * 1024 * 1024
        ),
        name="attention_backward",
    )(
        doc_lengths,
        plan,
        q_nope.reshape(layers, rows, head),
        q_rope[:, 0],
        grad_out.reshape(layers, rows, head),
        latent[0],
        key_rope[0],
        hidden_in[0],
        w_uk,
        w_uv,
    )
    return (
        dqn.reshape(q_nope.shape),
        dqr.reshape(q_rope.shape),
        dlat[None],
        dkr[None],
        dw,
    )


def solution(mesh):
    placed = (
        P(None, "dp", "cp", None, None),
        P(None, "dp", "cp", None),
        P(None, "dp", "cp", None, None),
        P("dp", "cp", None),
        P("dp", None, "cp"),
        P("dp", "cp", None),
        P(),
        P(),
        P("dp", None),
        P("dp", None, None),
    )
    return jax.shard_map(
        on_device,
        mesh=mesh,
        in_specs=placed,
        out_specs=(
            P(None, "dp", "cp", None, None),
            P(None, "dp", "cp", None),
            P("dp", "cp", None),
            P("dp", None, "cp"),
            P(("cp", "dp"), None),
        ),
        check_vma=False,
    )
```

```python
import functools
import math

import jax
import jax.numpy as jnp
from jax import lax
from jax.experimental import pallas as pl
from jax.experimental.pallas import tpu as pltpu
from jax.sharding import PartitionSpec as P

BF = jnp.bfloat16
F32 = jnp.float32
MESH = pl.DeviceIdType.MESH
MARGIN = 192
SUB = 64
WIN = 256
HG = 8
ROPE = 64
COLUMNS = (slice(0, 384), slice(384, 640))
PIECE = 64


def dot(a, b, ca, cb):
    return lax.dot_general(a, b, (((ca,), (cb,)), ((), ())), preferred_element_type=F32)


def each(count, body):
    def step(i, carry):
        body(i)
        return carry

    lax.fori_loop(0, count, step, 0)


def kernel(
    ncp, ndp, side,
    lens, plan, qn_h, qr_h, go_h, lat_h, kr_h, hid_h, wk_h, wv_h,
    dqn_h, dqr_h, dlat, dkr, dw,
    qn, qr, go, le, kr, hid, wk, wv, qf, gf, of, ro, ql, gl, dq, kept, bias, acc, on, orp,
    slab, ht, hr, back, back1, back2, joined, jr, part, parts,
    sem_q, sem_w, sem_k, sem_halo, sem_hs, sem_hr, sem_os, sem_or, sem_oo, sem_back,
    sem_near, sem_fwd_s, sem_fwd_r, sem_ps, sem_pr, sem_own,
):
    layers, rows, head = qn.shape
    tok = qr.shape[1]
    heads = rows // tok
    lat = gl.shape[3]
    ext = le.shape[1]
    steps = heads // HG
    blk = tok // ncp
    part_heads = heads // 2
    part_wide = part_heads * ROPE
    scale = 1.0 / math.sqrt(head + ROPE)
    c_me = lax.axis_index("cp")
    d_me = lax.axis_index("dp")

    def cp_dev(offset):
        return lax.rem(c_me + offset + ncp, ncp)

    def dp_dev(offset):
        return lax.rem(d_me + offset + ndp, ndp)

    def q_copies(layer):
        return [
            pltpu.make_async_copy(qn_h.at[layer], qn.at[layer], sem_q.at[layer, 0]),
            pltpu.make_async_copy(go_h.at[layer], go.at[layer], sem_q.at[layer, 1]),
            pltpu.make_async_copy(qr_h.at[layer], qr.at[layer], sem_q.at[layer, 2]),
        ]

    def w_copies(layer, step):
        heads_of = pl.ds(step * HG, HG)
        return [
            pltpu.make_async_copy(wk_h.at[layer, heads_of], wk.at[layer, heads_of], sem_w.at[layer, step, 0]),
            pltpu.make_async_copy(wv_h.at[layer, heads_of], wv.at[layer, heads_of], sem_w.at[layer, step, 1]),
        ]

    own_rows = slice(MARGIN, MARGIN + tok)
    edge = MARGIN - tok
    k_copies = [
        pltpu.make_async_copy(lat_h, le.at[own_rows, :lat], sem_k.at[0]),
        pltpu.make_async_copy(kr_h, kr, sem_k.at[1]),
        pltpu.make_async_copy(hid_h, hid, sem_k.at[2]),
    ]
    for c in k_copies:
        c.start()
    for layer in range(layers):
        for c in q_copies(layer):
            c.start()
        for step in range(steps):
            for c in w_copies(layer, step):
                c.start()

    barrier = pltpu.get_barrier_semaphore()

    def greet_cp(i):
        pl.semaphore_signal(barrier, inc=1, device_id=(cp_dev(i + 1), d_me), device_id_type=MESH)

    def greet_dp(i):
        pl.semaphore_signal(barrier, inc=1, device_id=(c_me, dp_dev(i + 1)), device_id_type=MESH)

    each(ncp - 1, greet_cp)
    each(ndp - 1, greet_dp)

    k_copies[0].wait()
    k_copies[1].wait()
    turned = kr[...].astype(F32)
    le[own_rows, lat:] = jnp.concatenate([turned, turned], axis=0).T.astype(BF)
    pl.semaphore_wait(barrier, ncp + ndp - 2)

    halo = [
        pltpu.make_async_remote_copy(
            le.at[own_rows], le.at[edge:MARGIN], sem_halo.at[0], sem_halo.at[1],
            device_id=(cp_dev(1), d_me), device_id_type=MESH,
        ),
        pltpu.make_async_remote_copy(
            le.at[MARGIN + tok - edge : MARGIN + tok], le.at[:edge], sem_halo.at[2], sem_halo.at[3],
            device_id=(cp_dev(2), d_me), device_id_type=MESH,
        ),
    ]
    for c in halo:
        c.start()

    k_copies[2].wait()
    width = hid.shape[1] // ncp
    rows_dev = width // ndp

    def turn(c):
        for j in range(width // 128):
            lanes = pl.ds(pl.multiple_of(c * width + j * 128, 128), 128)
            slab[j * 128 : j * 128 + 128, :] = hid[:, lanes].astype(F32).T
        pad = jnp.zeros((PIECE - rows_dev, tok), F32)
        for j in range(ndp):
            piece = jnp.concatenate([slab[j * rows_dev : (j + 1) * rows_dev, :], pad], axis=0)
            ht[j, pl.ds(pl.multiple_of(c * PIECE, PIECE), PIECE), :] = piece.astype(BF)

    each(ncp, turn)

    def my_lanes():
        return pl.ds(pl.multiple_of(d_me * tok, tok), tok)

    def hidden_copy(i):
        to = dp_dev(i + 1)
        return pltpu.make_async_remote_copy(
            ht.at[to], hr.at[:, my_lanes()], sem_hs.at[i], sem_hr.at[i],
            device_id=(c_me, to), device_id_type=MESH,
        )

    each(ndp - 1, lambda i: hidden_copy(i).start())
    hidden_own = pltpu.make_async_copy(ht.at[d_me], hr.at[:, my_lanes()], sem_own.at[0])
    hidden_own.start()

    acc[...] = jnp.zeros_like(acc)
    for s in range(2):
        t = c_me * tok + s * SUB + lax.broadcasted_iota(jnp.int32, (SUB, 128), 0)
        first = jnp.zeros((SUB, 128), jnp.int32)
        end = jnp.int32(0)
        for j in range(lens.shape[1]):
            end = end + lens[0, j]
            first = jnp.where(end <= t, end, first)
        for half in range(2):
            u = (
                c_me * tok - MARGIN + s * SUB + half * 128
                + lax.broadcasted_iota(jnp.int32, (SUB, 128), 1)
            )
            ok = (u >= first) & (u <= t)
            bias[s, :, half * 128 : half * 128 + 128] = jnp.where(ok, jnp.inf, -jnp.inf)
    low = lax.broadcasted_iota(jnp.int32, (SUB, 128), 1) < ROPE

    def out_parts(layer, half, to):
        tokens = pl.ds(pl.multiple_of(c_me * blk, blk), blk)
        return [
            (on.at[to, layer, half], dqn_h.at[layer, tokens, pl.ds(half * part_heads, part_heads)]),
            (orp.at[to, layer, half], dqr_h.at[layer, tokens, pl.ds(half * part_wide, part_wide)]),
        ]

    def out_copies(layer, half, i):
        to = cp_dev(i + 1)
        return [
            pltpu.make_async_remote_copy(
                src, dst, sem_os.at[layer, half, i, j], sem_or.at[layer, half, i, j],
                device_id=(to, d_me), device_id_type=MESH,
            )
            for j, (src, dst) in enumerate(out_parts(layer, half, to))
        ]

    def out_own(layer, half):
        return [
            pltpu.make_async_copy(src, dst, sem_oo.at[layer, half, j])
            for j, (src, dst) in enumerate(out_parts(layer, half, c_me))
        ]

    def widen(layer):
        for c in q_copies(layer):
            c.wait()

        def chunk(c):
            piece = pl.ds(pl.multiple_of(c * 512, 512), 512)
            qf[layer, piece, :] = qn[layer, piece, :].astype(F32)
            gf[layer, piece, :] = go[layer, piece, :].astype(F32)

        each(rows // 512, chunk)

    def absorb(n, slot, i):
        layer, step = n // steps, lax.rem(n, steps)
        h = step * HG + i
        a = dot(qf[layer, pl.ds(h, tok, stride=heads), :].astype(BF), wk[layer, h], 1, 0).astype(BF)
        b = dot(gf[layer, pl.ds(h, tok, stride=heads), :].astype(BF), wv[layer, h], 1, 1).astype(BF)
        lanes = pl.ds(pl.multiple_of((step * (HG // 2) + i // 2) * 128, 128), 128)
        mine = slice(i * SUB, i * SUB + SUB)
        for s in range(2):
            sub = slice(s * SUB, s * SUB + SUB)
            ql[slot, s, mine, :lat] = a[sub]
            gl[slot, s, mine, :] = b[sub]
            pair = qr[layer, sub, lanes].astype(F32)
            pair = jnp.where(low if i % 2 == 0 else ~low, pair, 0.0)
            ql[slot, s, mine, lat:] = pair.astype(BF)

    def scores(slot, s):
        win = slice(s * SUB, s * SUB + WIN)
        return dot(ql[slot, s], le[win, :], 1, 1), dot(gl[slot, s], le[win, :lat], 1, 1)

    def softmax(s, score, dprob, j):
        part_of = slice(j * 2 * SUB, (j + 1) * 2 * SUB)
        x = jnp.minimum(score[part_of].reshape(2, SUB, WIN), bias[s][None]).reshape(2 * SUB, WIN)
        e = jnp.exp((x - jnp.max(x, axis=1, keepdims=True)) * scale)
        d = dprob[part_of]
        inv = 1.0 / jnp.sum(e, axis=1, keepdims=True)
        delta = jnp.sum(e * d, axis=1, keepdims=True) * inv
        return (e * (inv * scale) * (d - delta)).astype(BF), (e * inv).astype(BF)

    def add_keys(slot, s, ds, low_p):
        win = slice(s * SUB, s * SUB + WIN)
        acc[win, :] += dot(ds, ql[slot, s], 0, 0)
        acc[win, :lat] += dot(low_p, gl[slot, s], 0, 0)

    def query_side(step, s, ds):
        win = slice(s * SUB, s * SUB + WIN)
        d = dot(ds, le[win, :], 1, 0)
        for i in range(HG):
            dq[i, s * SUB : s * SUB + SUB, :] = d[i * SUB : i * SUB + SUB, :lat].astype(BF)
        for j in range(HG // 2):
            even = d[2 * j * SUB : (2 * j + 1) * SUB, lat:]
            odd = d[(2 * j + 1) * SUB : (2 * j + 2) * SUB, lat:]
            both = jnp.where(low, even, odd).astype(BF)
            lanes = pl.ds(pl.multiple_of((lax.rem(step, 2) * (HG // 2) + j) * 128, 128), 128)
            for q in range(SUB // blk):
                ro[s * (SUB // blk) + q, :, lanes] = both[q * blk : q * blk + blk]

    def query_out(layer, step):
        for i in range(HG):
            back_q = dot(dq[i], wk[layer, step * HG + i], 1, 1)
            for q in range(ncp):
                of[q, pl.ds(lax.rem(step, 2) * HG + i, blk, stride=part_heads), :] = back_q[q * blk : q * blk + blk]

    def send_out(layer, half):
        def place(k):
            b = plan[0, c_me, k]
            on[k, layer, half] = of[b].astype(BF).reshape(blk, part_heads, head)
            orp[k, layer, half] = ro[b]

        each(ncp, place)

        def start(i):
            for c in out_copies(layer, half, i):
                c.start()

        each(ncp - 1, start)
        for c in out_own(layer, half):
            c.start()

    def step_body(n, layer, defer):
        slot = lax.rem(n, 2)
        follow = jnp.minimum(n + 1, layers * steps - 1)

        @pl.when(n + 1 < layers * steps)
        def _():
            for c in w_copies(follow // steps, lax.rem(follow, steps)):
                c.wait()

        step = n - layer * steps
        pend = None
        for s in range(2):
            score, dprob = scores(slot, s)
            if pend is not None:
                add_keys(slot, *pend)
                if not defer:
                    query_side(step, pend[0], pend[1])
            ds, low_p = [], []
            for j in range(HG // 2):
                x, p = softmax(s, score, dprob, j)
                ds.append(x)
                low_p.append(p)
                absorb(follow, 1 - slot, s * (HG // 2) + j)
            ds = jnp.concatenate(ds, axis=0)
            low_p = jnp.concatenate(low_p, axis=0)
            if defer:
                kept[step, s] = ds
            pend = (s, ds, low_p)
        add_keys(slot, *pend)
        if not defer:
            query_side(step, pend[0], pend[1])
            query_out(layer, step)

            @pl.when(lax.rem(step, 2) == 1)
            def _():
                send_out(layer, step // 2)

    back_copies = [
        pltpu.make_async_remote_copy(
            back.at[edge:MARGIN], back1, sem_back.at[0], sem_back.at[1],
            device_id=(cp_dev(-1), d_me), device_id_type=MESH,
        ),
        pltpu.make_async_remote_copy(
            back.at[:edge], back2, sem_back.at[2], sem_back.at[3],
            device_id=(cp_dev(-2), d_me), device_id_type=MESH,
        ),
    ]

    for layer in range(layers):
        widen(layer)
    for c in w_copies(0, 0):
        c.wait()
    for i in range(HG):
        absorb(jnp.int32(0), 0, i)
    for c in halo:
        c.wait_recv()

    last = layers - 1
    each(last * steps, lambda n: step_body(n, n // steps, False))
    each(steps, lambda n: step_body(n + last * steps, last, True))
    back[...] = acc[:MARGIN, :].astype(BF)
    for c in back_copies:
        c.start()

    def late_queries(step):
        for s in range(2):
            query_side(step, s, kept[step, s])
        query_out(last, step)

    each(2, late_queries)
    send_out(last, 0)

    for c in back_copies:
        c.wait_recv()
    total = acc[own_rows, :] + back1[...].astype(F32)
    late = total[tok - edge :] + back2[...].astype(F32)
    total = jnp.concatenate([total[: tok - edge], late], axis=0)
    rope = total[:, lat:]
    rope = rope + pltpu.roll(rope, ROPE, 1)
    low_all = lax.broadcasted_iota(jnp.int32, (tok, 128), 1) < ROPE
    rope = jnp.where(low_all, rope, 0.0)
    joined[:, :lat] = total[:, :lat].astype(BF)
    joined[:, lat:] = rope.astype(BF)
    dlat[...] = total[:, :lat].astype(BF)
    dkr[...] = rope.T[:ROPE].astype(BF)

    y, z = d_me // side, lax.rem(d_me, side)
    other = ndp // side
    half = tok // 2

    def place_of(yy, zz, which, ch):
        rows_of = pl.ds(pl.multiple_of((yy * side + zz) * tok + which * half, half), half)
        return jr.at[rows_of, COLUMNS[ch]]

    def ring(value, offset, n):
        return lax.rem(value + offset + n, n)

    def near(ch, which, k):
        lanes = COLUMNS[ch]
        src = joined.at[which * half : which * half + half, lanes]
        to = y * side + ring(z, k, side) if which == 0 else ring(y, k, other) * side + z
        return pltpu.make_async_remote_copy(
            src, place_of(y, z, which, ch), sem_near.at[ch, which, 0, k - 1], sem_near.at[ch, which, 1, k - 1],
            device_id=(c_me, to), device_id_type=MESH,
        )

    def forward(ch, which, j, k):
        if which == 0:
            ref = place_of(y, ring(z, -j, side), 0, ch)
            to = ring(y, k, other) * side + z
        else:
            ref = place_of(ring(y, -j, other), z, 1, ch)
            to = y * side + ring(z, k, side)
        src = joined.at[which * half : which * half + half, COLUMNS[ch]] if j == 0 else ref
        return pltpu.make_async_remote_copy(
            src, ref, sem_fwd_s.at[ch, which, j, k - 1], sem_fwd_r.at[ch, which, j, k - 1],
            device_id=(c_me, to), device_id_type=MESH,
        )

    for ch in range(len(COLUMNS)):
        for k in (1, 3, 2):
            near(ch, 0, k).start()
            near(ch, 1, k).start()
        for k in (1, 3, 2):
            forward(ch, 0, 0, k).start()
            forward(ch, 1, 0, k).start()
    gather_own = pltpu.make_async_copy(
        joined, jr.at[pl.ds(pl.multiple_of(d_me * tok, tok), tok)], sem_own.at[0]
    )
    hidden_own.wait()
    gather_own.start()
    each(2, lambda i: late_queries(i + 2))
    send_out(last, 1)
    for ch in range(len(COLUMNS)):
        for j in (1, 3, 2):
            for which in range(2):
                near(ch, which, j).wait_recv()
                for k in (1, 3, 2):
                    forward(ch, which, j, k).start()
    each(ndp - 1, lambda i: hidden_copy(i).wait())
    gather_own.wait()

    def part_copy(ch, i):
        to = cp_dev(i + 1)
        return pltpu.make_async_remote_copy(
            part.at[pl.ds(pl.multiple_of(to * PIECE, PIECE), PIECE), COLUMNS[ch]],
            parts.at[i, :, COLUMNS[ch]],
            sem_ps.at[ch, i], sem_pr.at[ch, i], device_id=(to, d_me), device_id_type=MESH,
        )

    for ch in range(len(COLUMNS)):
        for j in range(4):
            for which in range(2):
                for k in (1, 2, 3):
                    forward(ch, which, j, k).wait_recv()

        def product(c):
            piece = pl.ds(pl.multiple_of(c * 256, 256), 256)
            part[piece, COLUMNS[ch]] = dot(hr[piece, :], jr[:, COLUMNS[ch]], 1, 0).astype(BF)

        each(part.shape[0] // 256, product)
        each(ncp - 1, lambda i: part_copy(ch, i).start())
    for ch in range(len(COLUMNS)):
        cols = COLUMNS[ch]
        mine = part[pl.ds(pl.multiple_of(c_me * PIECE, PIECE), PIECE), cols].astype(F32)
        for i in range(ncp - 1):
            part_copy(ch, i).wait_recv()
            mine = mine + parts[i, :, cols].astype(F32)
        width_now = min(cols.stop, lat + ROPE) - cols.start
        dw[:, cols.start : cols.start + width_now] = mine[:rows_dev, :width_now]

    for c in halo + back_copies:
        c.wait_send()
    for ch in range(len(COLUMNS)):
        for which in range(2):
            for k in (1, 2, 3):
                near(ch, which, k).wait_send()
            for j in range(4):
                for k in (1, 2, 3):
                    forward(ch, which, j, k).wait_send()
        each(ncp - 1, lambda i: part_copy(ch, i).wait_send())

    def finish(n):
        layer, half = n // 2, lax.rem(n, 2)
        for c in out_own(layer, half):
            c.wait()

        def one(i):
            for c in out_copies(layer, half, i):
                c.wait()

        each(ncp - 1, one)

    each(2 * layers, finish)


def pass_on(*refs):
    count = (len(refs) - 2) // 3
    came, went = refs[-2:]
    moves = []
    for i in range(count):
        src, dst, held = refs[i], refs[count + i], refs[2 * count + i]
        pieces = [(0, slice(None))]
        if len(src.shape) > 2:
            cut = src.shape[1] // 4
            pieces = [(n, (n // 4, slice(n % 4 * cut, (n % 4 + 1) * cut))) for n in range(4 * src.shape[0])]
        for n, at in pieces:
            moves.append(
                (
                    pltpu.make_async_copy(src.at[at], held.at[at], came.at[i, n]),
                    pltpu.make_async_copy(held.at[at], dst.at[at], went.at[i, n]),
                )
            )
    for load, _ in moves:
        load.start()
    for load, store in moves:
        load.wait()
        store.start()
    for _, store in moves:
        store.wait()


def on_device(q_nope, q_rope, grad_out, latent, key_rope, hidden_in, w_uk, w_uv, doc_lengths, plan):
    ncp = lax.axis_size("cp")
    ndp = lax.axis_size("dp")
    side = math.isqrt(ndp)
    layers, _, tok, heads, head = q_nope.shape
    wide = q_rope.shape[3]
    lat = latent.shape[2]
    model = hidden_in.shape[2]
    ext = lat + 2 * ROPE
    rows = tok * heads
    smem = pl.BlockSpec(memory_space=pltpu.SMEM)
    hbm = pl.BlockSpec(memory_space=pl.ANY)
    vmem = pl.BlockSpec(memory_space=pltpu.VMEM)
    dma = pltpu.SemaphoreType.DMA
    results = pl.pallas_call(
        functools.partial(kernel, ncp, ndp, side),
        out_shape=(
            jax.ShapeDtypeStruct((layers, tok, heads, head), BF),
            jax.ShapeDtypeStruct((layers, tok, wide), BF),
            jax.ShapeDtypeStruct((tok, lat), BF),
            jax.ShapeDtypeStruct((ROPE, tok), BF),
            jax.ShapeDtypeStruct((model // (ncp * ndp), lat + ROPE), F32),
        ),
        in_specs=[smem, smem] + [hbm] * 8,
        out_specs=(hbm, hbm, vmem, vmem, vmem),
        scratch_shapes=[
            pltpu.VMEM((layers, rows, head), BF),
            pltpu.VMEM((layers, tok, wide), BF),
            pltpu.VMEM((layers, rows, head), BF),
            pltpu.VMEM((MARGIN + tok, ext), BF),
            pltpu.VMEM((ROPE, tok), BF),
            pltpu.VMEM((tok, model), BF),
            pltpu.VMEM(w_uk.shape, BF),
            pltpu.VMEM(w_uv.shape, BF),
            pltpu.VMEM((layers, rows, head), F32),
            pltpu.VMEM((layers, rows, head), F32),
            pltpu.VMEM((ncp, rows // ncp // 2, head), F32),
            pltpu.VMEM((ncp, tok // ncp, wide // 2), BF),
            pltpu.VMEM((2, 2, HG * SUB, ext), BF),
            pltpu.VMEM((2, 2, HG * SUB, lat), BF),
            pltpu.VMEM((HG, tok, lat), BF),
            pltpu.VMEM((heads // HG, 2, HG * SUB, WIN), BF),
            pltpu.VMEM((2, SUB, WIN), F32),
            pltpu.VMEM((MARGIN + tok, ext), F32),
            pltpu.VMEM((ncp, layers, 2, tok // ncp, heads // 2, head), BF),
            pltpu.VMEM((ncp, layers, 2, tok // ncp, wide // 2), BF),
            pltpu.VMEM((model // ncp, tok), F32),
            pltpu.VMEM((ndp, ncp * PIECE, tok), BF),
            pltpu.VMEM((ncp * PIECE, ndp * tok), BF),
            pltpu.VMEM((MARGIN, ext), BF),
            pltpu.VMEM((tok, ext), BF),
            pltpu.VMEM((MARGIN - tok, ext), BF),
            pltpu.VMEM((tok, ext), BF),
            pltpu.VMEM((ndp * tok, ext), BF),
            pltpu.VMEM((ncp * PIECE, ext), BF),
            pltpu.VMEM((ncp - 1, PIECE, ext), BF),
            dma((layers, 3)),
            dma((layers, heads // HG, 2)),
            dma((3,)),
            dma((4,)),
            dma((ndp - 1,)),
            dma((ndp - 1,)),
            dma((layers, 2, ncp - 1, 2)),
            dma((layers, 2, ncp - 1, 2)),
            dma((layers, 2, 2)),
            dma((4,)),
            dma((len(COLUMNS), 2, 2, 3)),
            dma((len(COLUMNS), 2, 4, 3)),
            dma((len(COLUMNS), 2, 4, 3)),
            dma((len(COLUMNS), ncp - 1)),
            dma((len(COLUMNS), ncp - 1)),
            dma((1,)),
        ],
        compiler_params=pltpu.CompilerParams(
            collective_id=0, has_side_effects=True, vmem_limit_bytes=60 * 1024 * 1024
        ),
        name="attention_backward",
    )(
        doc_lengths,
        plan,
        q_nope.reshape(layers, rows, head),
        q_rope[:, 0],
        grad_out.reshape(layers, rows, head),
        latent[0],
        key_rope[0],
        hidden_in[0],
        w_uk,
        w_uv,
    )
    dqn, dqr, dlat, dkr, dw = pl.pallas_call(
        pass_on,
        out_shape=tuple(jax.ShapeDtypeStruct(r.shape, r.dtype) for r in results),
        in_specs=[hbm] * 5,
        out_specs=(hbm,) * 5,
        scratch_shapes=[pltpu.VMEM(r.shape, r.dtype) for r in results] + [dma((5, 8)), dma((5, 8))],
        name="pass_on",
    )(*results)
    return (
        dqn.reshape(q_nope.shape),
        dqr.reshape(q_rope.shape),
        dlat[None],
        dkr[None],
        dw,
    )


def solution(mesh):
    placed = (
        P(None, "dp", "cp", None, None),
        P(None, "dp", "cp", None),
        P(None, "dp", "cp", None, None),
        P("dp", "cp", None),
        P("dp", None, "cp"),
        P("dp", "cp", None),
        P(),
        P(),
        P("dp", None),
        P("dp", None, None),
    )
    return jax.shard_map(
        on_device,
        mesh=mesh,
        in_specs=placed,
        out_specs=(
            P(None, "dp", "cp", None, None),
            P(None, "dp", "cp", None),
            P("dp", "cp", None),
            P("dp", None, "cp"),
            P(("cp", "dp"), None),
        ),
        check_vma=False,
    )
```

```python
import functools
import math

import jax
import jax.numpy as jnp
from jax import lax
from jax.experimental import pallas as pl
from jax.experimental.pallas import tpu as pltpu
from jax.sharding import PartitionSpec as P

BF = jnp.bfloat16
F32 = jnp.float32
MESH = pl.DeviceIdType.MESH
MARGIN = 192
SUB = 64
WIN = 256
HG = 8
PITCH = 36
OUT_PITCH = 20
ROPE = 64
FIRST = 384
PIECE = 64


def dot(a, b, ca, cb):
    return lax.dot_general(a, b, (((ca,), (cb,)), ((), ())), preferred_element_type=F32)


def each(count, body):
    def step(i, carry):
        body(i)
        return carry

    lax.fori_loop(0, count, step, 0)


def kernel(
    ncp, ndp, side,
    lens, plan, qn_h, qr_h, go_h, lat_h, kr_h, hid_h, wk_h, wv_h,
    dqn_h, dqr_h, dlat, dkr, dw,
    qn, qr, go, le, kr, hid, wk, wv, qf, gf, of, ro, ql, gl, dq, kept, bias, acc, on, orp,
    slab, ht, hr, back, back1, back2, ja, jb, ga, gb, gc, pa, pb, ra, rb,
    sem_q, sem_w, sem_k, sem_halo, sem_hs, sem_hr, sem_os, sem_or, sem_oo, sem_back,
    sem_near, sem_fwd_s, sem_fwd_r, sem_rel, sem_ps, sem_pr, sem_own,
):
    layers, rows, head = qn.shape
    tok = qr.shape[1]
    heads = rows // tok
    lat = gl.shape[3]
    ext = le.shape[1]
    steps = heads // HG
    blk = tok // ncp
    part_heads = heads // 2
    part_wide = part_heads * ROPE
    scale = 1.0 / math.sqrt(head + ROPE)
    c_me = lax.axis_index("cp")
    d_me = lax.axis_index("dp")

    def cp_dev(offset):
        return lax.rem(c_me + offset + ncp, ncp)

    def dp_dev(offset):
        return lax.rem(d_me + offset + ndp, ndp)

    def q_copies(layer):
        return [
            pltpu.make_async_copy(qn_h.at[layer], qn.at[layer], sem_q.at[layer, 0]),
            pltpu.make_async_copy(go_h.at[layer], go.at[layer], sem_q.at[layer, 1]),
            pltpu.make_async_copy(qr_h.at[layer], qr.at[layer], sem_q.at[layer, 2]),
        ]

    def w_copies(layer, step):
        heads_of = pl.ds(step * HG, HG)
        return [
            pltpu.make_async_copy(wk_h.at[layer, heads_of], wk.at[layer, heads_of], sem_w.at[layer, step, 0]),
            pltpu.make_async_copy(wv_h.at[layer, heads_of], wv.at[layer, heads_of], sem_w.at[layer, step, 1]),
        ]

    own_rows = slice(MARGIN, MARGIN + tok)
    edge = MARGIN - tok
    k_copies = [
        pltpu.make_async_copy(lat_h, le.at[own_rows, :lat], sem_k.at[0]),
        pltpu.make_async_copy(kr_h, kr, sem_k.at[1]),
        pltpu.make_async_copy(hid_h, hid, sem_k.at[2]),
    ]
    for c in k_copies[:2] + q_copies(0) + w_copies(0, 0):
        c.start()

    barrier = pltpu.get_barrier_semaphore()

    def greet_cp(i):
        pl.semaphore_signal(barrier, inc=1, device_id=(cp_dev(i + 1), d_me), device_id_type=MESH)

    def greet_dp(i):
        pl.semaphore_signal(barrier, inc=1, device_id=(c_me, dp_dev(i + 1)), device_id_type=MESH)

    each(ncp - 1, greet_cp)
    each(ndp - 1, greet_dp)

    k_copies[0].wait()
    k_copies[1].wait()
    turned = kr[...].astype(F32)
    le[own_rows, lat:] = jnp.concatenate([turned, turned], axis=0).T.astype(BF)
    pl.semaphore_wait(barrier, ncp + ndp - 2)

    halo = [
        pltpu.make_async_remote_copy(
            le.at[own_rows], le.at[edge:MARGIN], sem_halo.at[0], sem_halo.at[1],
            device_id=(cp_dev(1), d_me), device_id_type=MESH,
        ),
        pltpu.make_async_remote_copy(
            le.at[MARGIN + tok - edge : MARGIN + tok], le.at[:edge], sem_halo.at[2], sem_halo.at[3],
            device_id=(cp_dev(2), d_me), device_id_type=MESH,
        ),
    ]
    for c in halo:
        c.start()

    acc[...] = jnp.zeros_like(acc)
    for s in range(2):
        t = c_me * tok + s * SUB + lax.broadcasted_iota(jnp.int32, (SUB, 128), 0)
        first = jnp.zeros((SUB, 128), jnp.int32)
        end = jnp.int32(0)
        for j in range(lens.shape[1]):
            end = end + lens[0, j]
            first = jnp.where(end <= t, end, first)
        for half in range(2):
            u = (
                c_me * tok - MARGIN + s * SUB + half * 128
                + lax.broadcasted_iota(jnp.int32, (SUB, 128), 1)
            )
            ok = (u >= first) & (u <= t)
            bias[s, :, half * 128 : half * 128 + 128] = jnp.where(ok, jnp.inf, -jnp.inf)
    low = lax.broadcasted_iota(jnp.int32, (SUB, 128), 1) < ROPE

    def out_parts(layer, half, to):
        tokens = pl.ds(pl.multiple_of(c_me * blk, blk), blk)
        return [
            (on.at[to, layer, half], dqn_h.at[layer, tokens, pl.ds(half * part_heads, part_heads)]),
            (orp.at[to, layer, half], dqr_h.at[layer, tokens, pl.ds(half * part_wide, part_wide)]),
        ]

    def out_copies(layer, half, i):
        to = cp_dev(i + 1)
        return [
            pltpu.make_async_remote_copy(
                src, dst, sem_os.at[layer, half, i, j], sem_or.at[layer, half, i, j],
                device_id=(to, d_me), device_id_type=MESH,
            )
            for j, (src, dst) in enumerate(out_parts(layer, half, to))
        ]

    def out_own(layer, half):
        return [
            pltpu.make_async_copy(src, dst, sem_oo.at[layer, half, j])
            for j, (src, dst) in enumerate(out_parts(layer, half, c_me))
        ]

    def widen(layer):
        for c in q_copies(layer):
            c.wait()

        def chunk(c):
            piece = pl.ds(pl.multiple_of(c * blk * heads, blk * heads), blk * heads)
            for wide_ref, ref in ((qf, qn), (gf, go)):
                value = ref[layer, piece, :].astype(F32)
                for t in range(blk):
                    at = pl.ds(c * (blk * PITCH) + t * PITCH, heads)
                    wide_ref[layer, at, :] = value[t * heads : (t + 1) * heads]

        each(tok // blk, chunk)

    def absorb(n, slot, i):
        layer, step = n // steps, lax.rem(n, steps)
        h = step * HG + i
        a = dot(qf[layer, pl.ds(h, tok, stride=PITCH), :].astype(BF), wk[layer, h], 1, 0).astype(BF)
        b = dot(gf[layer, pl.ds(h, tok, stride=PITCH), :].astype(BF), wv[layer, h], 1, 1).astype(BF)
        lanes = pl.ds(pl.multiple_of((step * (HG // 2) + i // 2) * 128, 128), 128)
        mine = slice(i * SUB, i * SUB + SUB)
        for s in range(2):
            sub = slice(s * SUB, s * SUB + SUB)
            ql[slot, s, mine, :lat] = a[sub]
            gl[slot, s, mine, :] = b[sub]
            pair = qr[layer, sub, lanes].astype(F32)
            pair = jnp.where(low if i % 2 == 0 else ~low, pair, 0.0)
            ql[slot, s, mine, lat:] = pair.astype(BF)

    def scores(slot, s):
        win = slice(s * SUB, s * SUB + WIN)
        return dot(ql[slot, s], le[win, :], 1, 1), dot(gl[slot, s], le[win, :lat], 1, 1)

    def softmax(s, score, dprob, j):
        part_of = slice(j * 2 * SUB, (j + 1) * 2 * SUB)
        x = jnp.minimum(score[part_of].reshape(2, SUB, WIN), bias[s][None]).reshape(2 * SUB, WIN)
        e = jnp.exp((x - jnp.max(x, axis=1, keepdims=True)) * scale)
        d = dprob[part_of]
        inv = 1.0 / jnp.sum(e, axis=1, keepdims=True)
        delta = jnp.sum(e * d, axis=1, keepdims=True) * inv
        return (e * (inv * scale) * (d - delta)).astype(BF), (e * inv).astype(BF)

    def add_keys(slot, s, ds, low_p):
        win = slice(s * SUB, s * SUB + WIN)
        acc[win, :] += dot(ds, ql[slot, s], 0, 0)
        acc[win, :lat] += dot(low_p, gl[slot, s], 0, 0)

    def query_side(step, s, ds):
        win = slice(s * SUB, s * SUB + WIN)
        d = dot(ds, le[win, :], 1, 0)
        for i in range(HG):
            dq[i, s * SUB : s * SUB + SUB, :] = d[i * SUB : i * SUB + SUB, :lat].astype(BF)
        for j in range(HG // 2):
            even = d[2 * j * SUB : (2 * j + 1) * SUB, lat:]
            odd = d[(2 * j + 1) * SUB : (2 * j + 2) * SUB, lat:]
            both = jnp.where(low, even, odd).astype(BF)
            lanes = pl.ds(pl.multiple_of((lax.rem(step, 2) * (HG // 2) + j) * 128, 128), 128)
            for q in range(SUB // blk):
                ro[s * (SUB // blk) + q, :, lanes] = both[q * blk : q * blk + blk]

    def query_out(layer, step):
        for i in range(HG):
            back_q = dot(dq[i], wk[layer, step * HG + i], 1, 1)
            for q in range(ncp):
                of[q, pl.ds(lax.rem(step, 2) * HG + i, blk, stride=OUT_PITCH), :] = back_q[q * blk : q * blk + blk]

    def send_out(layer, half):
        def place(k):
            b = plan[0, c_me, k]
            for t in range(blk):
                on[k, layer, half, t] = of[b, t * OUT_PITCH : t * OUT_PITCH + part_heads, :].astype(BF)
            orp[k, layer, half] = ro[b]

        each(ncp, place)

        def start(i):
            for c in out_copies(layer, half, i):
                c.start()

        each(ncp - 1, start)
        for c in out_own(layer, half):
            c.start()

    def step_body(n, layer, defer, more):
        slot = lax.rem(n, 2)
        follow = n + 1
        step = n - layer * steps
        if not defer:

            @pl.when(step == 1)
            def _():
                widen(layer + 1)

        if more:
            ahead = n + 3

            @pl.when(ahead < layers * steps)
            def _():
                for c in w_copies(ahead // steps, lax.rem(ahead, steps)):
                    c.start()

            for c in w_copies(follow // steps, lax.rem(follow, steps)):
                c.wait()

        pend = None
        for s in range(2):
            score, dprob = scores(slot, s)
            if pend is not None:
                add_keys(slot, *pend)
                if not defer:
                    query_side(step, pend[0], pend[1])
            ds, low_p = [], []
            for j in range(HG // 2):
                x, p = softmax(s, score, dprob, j)
                ds.append(x)
                low_p.append(p)
                if more:
                    absorb(follow, 1 - slot, s * (HG // 2) + j)
            ds = jnp.concatenate(ds, axis=0)
            low_p = jnp.concatenate(low_p, axis=0)
            if defer:
                kept[step, s] = ds
            pend = (s, ds, low_p)
        add_keys(slot, *pend)
        if not defer:
            query_side(step, pend[0], pend[1])
            query_out(layer, step)

            @pl.when(lax.rem(step, 2) == 1)
            def _():
                send_out(layer, step // 2)

    back_copies = [
        pltpu.make_async_remote_copy(
            back.at[edge:MARGIN], back1, sem_back.at[0], sem_back.at[1],
            device_id=(cp_dev(-1), d_me), device_id_type=MESH,
        ),
        pltpu.make_async_remote_copy(
            back.at[:edge], back2, sem_back.at[2], sem_back.at[3],
            device_id=(cp_dev(-2), d_me), device_id_type=MESH,
        ),
    ]

    widen(0)
    for c in k_copies[2:] + w_copies(0, 1):
        c.start()
    for c in w_copies(0, 0):
        c.wait()
    for c in q_copies(1) + w_copies(0, 2):
        c.start()
    for i in range(HG):
        absorb(jnp.int32(0), 0, i)

    k_copies[2].wait()
    width = hid.shape[1] // ncp
    rows_dev = width // ndp

    def turn(c):
        for j in range(width // 128):
            lanes = pl.ds(pl.multiple_of(c * width + j * 128, 128), 128)
            slab[j * 128 : j * 128 + 128, :] = hid[:, lanes].astype(F32).T
        pad = jnp.zeros((PIECE - rows_dev, tok), F32)
        for j in range(ndp):
            piece = jnp.concatenate([slab[j * rows_dev : (j + 1) * rows_dev, :], pad], axis=0)
            ht[j, pl.ds(pl.multiple_of(c * PIECE, PIECE), PIECE), :] = piece.astype(BF)

    each(ncp, turn)

    def my_lanes():
        return pl.ds(pl.multiple_of(d_me * tok, tok), tok)

    def hidden_copy(i):
        to = dp_dev(i + 1)
        return pltpu.make_async_remote_copy(
            ht.at[to], hr.at[:, my_lanes()], sem_hs.at[i], sem_hr.at[i],
            device_id=(c_me, to), device_id_type=MESH,
        )

    each(ndp - 1, lambda i: hidden_copy(i).start())
    hidden_own = pltpu.make_async_copy(ht.at[d_me], hr.at[:, my_lanes()], sem_own.at[0])
    hidden_own.start()

    for c in halo:
        c.wait_recv()

    last = layers - 1
    each(last * steps, lambda n: step_body(n, n // steps, False, True))
    each(steps - 1, lambda n: step_body(n + last * steps, last, True, True))
    step_body(jnp.int32(layers * steps - 1), last, True, False)
    back[...] = acc[:MARGIN, :].astype(BF)
    for c in back_copies:
        c.start()

    def late_queries(step):
        for s in range(2):
            query_side(step, s, kept[step, s])
        query_out(last, step)

    each(2, late_queries)
    send_out(last, 0)

    for c in back_copies:
        c.wait_recv()
    total = acc[own_rows, :] + back1[...].astype(F32)
    late = total[tok - edge :] + back2[...].astype(F32)
    total = jnp.concatenate([total[: tok - edge], late], axis=0)
    rope = total[:, lat:]
    rope = rope + pltpu.roll(rope, ROPE, 1)
    low_all = lax.broadcasted_iota(jnp.int32, (tok, 128), 1) < ROPE
    rope = jnp.where(low_all, rope, 0.0)
    half = tok // 2
    quarter = half // 2
    for w in range(2):
        of_half = slice(w * half, w * half + half)
        ja[of_half, :] = total[of_half, :FIRST].astype(BF)
        jb[w, :half, :] = total[of_half, FIRST:lat].astype(BF)
        top = rope[w * half : w * half + quarter]
        bottom = pltpu.roll(rope[w * half + quarter : (w + 1) * half], ROPE, 1)
        jb[w, half:, :] = (top + bottom).astype(BF)
    dlat[...] = total[:, :lat].astype(BF)
    dkr[...] = rope.T[:ROPE].astype(BF)

    y, z = d_me // side, lax.rem(d_me, side)
    other = ndp // side

    def place_of(yy, zz, which, ch):
        if ch == 1:
            return gb.at[yy * side + zz, which]
        return ga.at[pl.ds(pl.multiple_of((yy * side + zz) * tok + which * half, half), half)]

    def mine_of(which, ch):
        return jb.at[which] if ch == 1 else ja.at[which * half : which * half + half]

    def ring(value, offset, n):
        return lax.rem(value + offset + n, n)

    def near(ch, which, k):
        src = mine_of(which, ch)
        to = y * side + ring(z, k, side) if which == 0 else ring(y, k, other) * side + z
        return pltpu.make_async_remote_copy(
            src, place_of(y, z, which, ch), sem_near.at[ch, which, 0, k - 1], sem_near.at[ch, which, 1, k - 1],
            device_id=(c_me, to), device_id_type=MESH,
        )

    def forward(ch, which, j, k):
        if which == 0:
            ref = place_of(y, ring(z, -j, side), 0, ch)
            to = ring(y, k, other) * side + z
        else:
            ref = place_of(ring(y, -j, other), z, 1, ch)
            to = y * side + ring(z, k, side)
        src = mine_of(which, ch) if j == 0 else ref
        return pltpu.make_async_remote_copy(
            src, ref, sem_fwd_s.at[ch, which, j, k - 1], sem_fwd_r.at[ch, which, j, k - 1],
            device_id=(c_me, to), device_id_type=MESH,
        )

    def relay(which, j, back_by):
        step = 1 if back_by == 0 else -1
        if which == 0:
            ref = place_of(ring(y, -step, other), ring(z, -j, side), 0, 0)
            to = ring(y, step, other) * side + z
        else:
            ref = place_of(ring(y, -j, other), ring(z, -step, side), 1, 0)
            to = y * side + ring(z, step, side)
        ref = ref.at[pl.ds(back_by * quarter, quarter)]
        return pltpu.make_async_remote_copy(
            ref, ref, sem_rel.at[which, j, back_by, 0], sem_rel.at[which, j, back_by, 1],
            device_id=(c_me, to), device_id_type=MESH,
        )

    for ch in range(2):
        for k in (1, 3, 2):
            near(ch, 0, k).start()
            near(ch, 1, k).start()
        for k in (1, 3) if ch == 0 else (1, 3, 2):
            forward(ch, 0, 0, k).start()
            forward(ch, 1, 0, k).start()
    gather_own = [
        pltpu.make_async_copy(ja, ga.at[pl.ds(pl.multiple_of(d_me * tok, tok), tok)], sem_own.at[0]),
        pltpu.make_async_copy(jb, gb.at[d_me], sem_own.at[1]),
    ]
    hidden_own.wait()
    for c in gather_own:
        c.start()
    each(2, lambda i: late_queries(i + 2))
    send_out(last, 1)
    for j in (1, 3, 2):
        for which in range(2):
            near(0, which, j).wait_recv()
            for k in (1, 3):
                forward(0, which, j, k).start()
    for j in (0, 1, 3, 2):
        for which in range(2):
            for k in (1, 3):
                forward(0, which, j, k).wait_recv()
                relay(which, j, k // 2).start()
    for j in (1, 3, 2):
        for which in range(2):
            near(1, which, j).wait_recv()
            for k in (1, 3, 2):
                forward(1, which, j, k).start()
    each(ndp - 1, lambda i: hidden_copy(i).wait())
    for c in gather_own:
        c.wait()
    for j in (0, 1, 3, 2):
        for which in range(2):
            for back_by in range(2):
                relay(which, j, back_by).wait_recv()

    def part_copy(ch, i):
        to = cp_dev(i + 1)
        src, dst = ((pa, ra), (pb, rb))[ch]
        return pltpu.make_async_remote_copy(
            src.at[to], dst.at[i], sem_ps.at[ch, i], sem_pr.at[ch, i],
            device_id=(to, d_me), device_id_type=MESH,
        )

    block = 4 * PIECE

    def product(c):
        d = dot(hr[pl.ds(pl.multiple_of(c * block, block), block), :], ga[...], 1, 0).astype(BF)
        for i in range(4):
            pa[c * 4 + i] = d[i * PIECE : (i + 1) * PIECE]

    each(ncp // 4, product)
    each(ncp - 1, lambda i: part_copy(0, i).start())
    for j in range(4):
        for which in range(2):
            for k in (1, 2, 3):
                forward(1, which, j, k).wait_recv()

    def unfold(i):
        for w in range(2):
            at = i * tok + w * half
            gc[pl.ds(pl.multiple_of(at, half), half), :128] = gb[i, w, :half, :]
            folded = gb[i, w, half:, :].astype(F32)
            gc[pl.ds(pl.multiple_of(at, quarter), quarter), 128:] = folded.astype(BF)
            gc[pl.ds(pl.multiple_of(at + quarter, quarter), quarter), 128:] = pltpu.roll(folded, ROPE, 1).astype(BF)

    each(ndp, unfold)

    def product_rest(c):
        d = dot(hr[pl.ds(pl.multiple_of(c * block, block), block), :], gc[...], 1, 0)
        for i in range(4):
            piece = d[i * PIECE : (i + 1) * PIECE]
            pb[c * 4 + i, :PIECE, :] = piece[:, :128].astype(BF)
            folded = jnp.where(low[: PIECE // 2], piece[: PIECE // 2, 128:], pltpu.roll(piece[PIECE // 2 :, 128:], ROPE, 1))
            pb[c * 4 + i, PIECE:, :] = folded.astype(BF)

    each(ncp // 4, product_rest)
    each(ncp - 1, lambda i: part_copy(1, i).start())
    for c in halo + back_copies:
        c.wait_send()
    for which in range(2):
        for ch in range(2):
            for k in (1, 2, 3):
                near(ch, which, k).wait_send()
            for j in range(4):
                for k in (1, 3) if ch == 0 else (1, 2, 3):
                    forward(ch, which, j, k).wait_send()
        for j in range(4):
            for back_by in range(2):
                relay(which, j, back_by).wait_send()
    first = pa[c_me].astype(F32)
    for i in range(ncp - 1):
        part_copy(0, i).wait_recv()
        first = first + ra[i].astype(F32)
    dw[:, :FIRST] = first[:rows_dev]
    rest = pb[c_me].astype(F32)
    for i in range(ncp - 1):
        part_copy(1, i).wait_recv()
        rest = rest + rb[i].astype(F32)
    dw[:, FIRST:lat] = rest[:rows_dev]
    dw[: PIECE // 2, lat:] = rest[PIECE:, :ROPE]
    dw[PIECE // 2 :, lat:] = pltpu.roll(rest[PIECE:], ROPE, 1)[: rows_dev - PIECE // 2, :ROPE]

    for ch in range(2):
        each(ncp - 1, lambda i: part_copy(ch, i).wait_send())

    def finish(n):
        layer, half = n // 2, lax.rem(n, 2)
        for c in out_own(layer, half):
            c.wait()

        def one(i):
            for c in out_copies(layer, half, i):
                c.wait()

        each(ncp - 1, one)

    each(2 * layers, finish)


def pass_on(*refs):
    count = (len(refs) - 2) // 3
    came, went = refs[-2:]
    moves = []
    for i in range(count):
        src, dst, held = refs[i], refs[count + i], refs[2 * count + i]
        pieces = [(0, slice(None))]
        if len(src.shape) > 2:
            cut = src.shape[1] // 4
            pieces = [(n, (n // 4, slice(n % 4 * cut, (n % 4 + 1) * cut))) for n in range(4 * src.shape[0])]
        for n, at in pieces:
            moves.append(
                (
                    pltpu.make_async_copy(src.at[at], held.at[at], came.at[i, n]),
                    pltpu.make_async_copy(held.at[at], dst.at[at], went.at[i, n]),
                )
            )
    for load, _ in moves:
        load.start()
    for load, store in moves:
        load.wait()
        store.start()
    for _, store in moves:
        store.wait()


def on_device(q_nope, q_rope, grad_out, latent, key_rope, hidden_in, w_uk, w_uv, doc_lengths, plan):
    ncp = lax.axis_size("cp")
    ndp = lax.axis_size("dp")
    side = math.isqrt(ndp)
    layers, _, tok, heads, head = q_nope.shape
    wide = q_rope.shape[3]
    lat = latent.shape[2]
    model = hidden_in.shape[2]
    ext = lat + 2 * ROPE
    rows = tok * heads
    smem = pl.BlockSpec(memory_space=pltpu.SMEM)
    hbm = pl.BlockSpec(memory_space=pl.ANY)
    vmem = pl.BlockSpec(memory_space=pltpu.VMEM)
    dma = pltpu.SemaphoreType.DMA
    results = pl.pallas_call(
        functools.partial(kernel, ncp, ndp, side),
        out_shape=(
            jax.ShapeDtypeStruct((layers, tok, heads, head), BF),
            jax.ShapeDtypeStruct((layers, tok, wide), BF),
            jax.ShapeDtypeStruct((tok, lat), BF),
            jax.ShapeDtypeStruct((ROPE, tok), BF),
            jax.ShapeDtypeStruct((model // (ncp * ndp), lat + ROPE), F32),
        ),
        in_specs=[smem, smem] + [hbm] * 8,
        out_specs=(hbm, hbm, vmem, vmem, vmem),
        scratch_shapes=[
            pltpu.VMEM((layers, rows, head), BF),
            pltpu.VMEM((layers, tok, wide), BF),
            pltpu.VMEM((layers, rows, head), BF),
            pltpu.VMEM((MARGIN + tok, ext), BF),
            pltpu.VMEM((ROPE, tok), BF),
            pltpu.VMEM((tok, model), BF),
            pltpu.VMEM(w_uk.shape, BF),
            pltpu.VMEM(w_uv.shape, BF),
            pltpu.VMEM((layers, tok * PITCH, head), F32),
            pltpu.VMEM((layers, tok * PITCH, head), F32),
            pltpu.VMEM((ncp, tok // ncp * OUT_PITCH, head), F32),
            pltpu.VMEM((ncp, tok // ncp, wide // 2), BF),
            pltpu.VMEM((2, 2, HG * SUB, ext), BF),
            pltpu.VMEM((2, 2, HG * SUB, lat), BF),
            pltpu.VMEM((HG, tok, lat), BF),
            pltpu.VMEM((heads // HG, 2, HG * SUB, WIN), BF),
            pltpu.VMEM((2, SUB, WIN), F32),
            pltpu.VMEM((MARGIN + tok, ext), F32),
            pltpu.VMEM((ncp, layers, 2, tok // ncp, heads // 2, head), BF),
            pltpu.VMEM((ncp, layers, 2, tok // ncp, wide // 2), BF),
            pltpu.VMEM((model // ncp, tok), F32),
            pltpu.VMEM((ndp, ncp * PIECE, tok), BF),
            pltpu.VMEM((ncp * PIECE, ndp * tok), BF),
            pltpu.VMEM((MARGIN, ext), BF),
            pltpu.VMEM((tok, ext), BF),
            pltpu.VMEM((MARGIN - tok, ext), BF),
            pltpu.VMEM((tok, FIRST), BF),
            pltpu.VMEM((2, tok // 2 + tok // 4, 128), BF),
            pltpu.VMEM((ndp * tok, FIRST), BF),
            pltpu.VMEM((ndp, 2, tok // 2 + tok // 4, 128), BF),
            pltpu.VMEM((ndp * tok, 256), BF),
            pltpu.VMEM((ncp, PIECE, FIRST), BF),
            pltpu.VMEM((ncp, PIECE + PIECE // 2, 128), BF),
            pltpu.VMEM((ncp - 1, PIECE, FIRST), BF),
            pltpu.VMEM((ncp - 1, PIECE + PIECE // 2, 128), BF),
            dma((layers, 3)),
            dma((layers, heads // HG, 2)),
            dma((3,)),
            dma((4,)),
            dma((ndp - 1,)),
            dma((ndp - 1,)),
            dma((layers, 2, ncp - 1, 2)),
            dma((layers, 2, ncp - 1, 2)),
            dma((layers, 2, 2)),
            dma((4,)),
            dma((2, 2, 2, 3)),
            dma((2, 2, 4, 3)),
            dma((2, 2, 4, 3)),
            dma((2, 4, 2, 2)),
            dma((2, ncp - 1)),
            dma((2, ncp - 1)),
            dma((2,)),
        ],
        compiler_params=pltpu.CompilerParams(
            collective_id=0, has_side_effects=True, vmem_limit_bytes=60 * 1024 * 1024
        ),
        name="attention_backward",
    )(
        doc_lengths,
        plan,
        q_nope.reshape(layers, rows, head),
        q_rope[:, 0],
        grad_out.reshape(layers, rows, head),
        latent[0],
        key_rope[0],
        hidden_in[0],
        w_uk,
        w_uv,
    )
    dqn, dqr, dlat, dkr, dw = pl.pallas_call(
        pass_on,
        out_shape=tuple(jax.ShapeDtypeStruct(r.shape, r.dtype) for r in results),
        in_specs=[hbm] * 5,
        out_specs=(hbm,) * 5,
        scratch_shapes=[pltpu.VMEM(r.shape, r.dtype) for r in results] + [dma((5, 8)), dma((5, 8))],
        name="pass_on",
    )(*results)
    return (
        dqn.reshape(q_nope.shape),
        dqr.reshape(q_rope.shape),
        dlat[None],
        dkr[None],
        dw,
    )


def solution(mesh):
    placed = (
        P(None, "dp", "cp", None, None),
        P(None, "dp", "cp", None),
        P(None, "dp", "cp", None, None),
        P("dp", "cp", None),
        P("dp", None, "cp"),
        P("dp", "cp", None),
        P(),
        P(),
        P("dp", None),
        P("dp", None, None),
    )
    return jax.shard_map(
        on_device,
        mesh=mesh,
        in_specs=placed,
        out_specs=(
            P(None, "dp", "cp", None, None),
            P(None, "dp", "cp", None),
            P("dp", "cp", None),
            P("dp", None, "cp"),
            P(("cp", "dp"), None),
        ),
        check_vma=False,
    )
```

```python
import functools
import math

import jax
import jax.numpy as jnp
from jax import lax
from jax.experimental import pallas as pl
from jax.experimental.pallas import tpu as pltpu
from jax.sharding import PartitionSpec as P

BF = jnp.bfloat16
F32 = jnp.float32
MESH = pl.DeviceIdType.MESH
MARGIN = 192
SUB = 64
WIN = 256
HG = 8
PITCH = 36
OUT_PITCH = 20
ROPE = 64
FIRST = 384
PIECE = 64


def dot(a, b, ca, cb):
    return lax.dot_general(a, b, (((ca,), (cb,)), ((), ())), preferred_element_type=F32)


def each(count, body):
    def step(i, carry):
        body(i)
        return carry

    lax.fori_loop(0, count, step, 0)


def kernel(
    ncp, ndp, side,
    lens, plan, qn_h, qr_h, go_h, lat_h, kr_h, hid_h, wk_h, wv_h,
    dqn_h, dqr_h, dlat, dkr, dw,
    qn, qr, go, le, kr, hid, wk, wv, qf, gf, of, ro, ql, gl, dq, kept, bias, acc, on, orp,
    slab, ht, hr, back, back1, back2, ja, jb, ga, gb, gc, pa, pb, ra, rb,
    sem_q, sem_w, sem_k, sem_halo, sem_hs, sem_hr, sem_os, sem_or, sem_oo, sem_back,
    sem_near, sem_fwd_s, sem_fwd_r, sem_rel, sem_ps, sem_pr, sem_own,
):
    layers, rows, head = qn.shape
    tok = qr.shape[1]
    heads = rows // tok
    lat = gl.shape[3]
    ext = le.shape[1]
    steps = heads // HG
    blk = tok // ncp
    part_heads = heads // 2
    part_wide = part_heads * ROPE
    scale = 1.0 / math.sqrt(head + ROPE)
    c_me = lax.axis_index("cp")
    d_me = lax.axis_index("dp")

    def cp_dev(offset):
        return lax.rem(c_me + offset + ncp, ncp)

    def dp_dev(offset):
        return lax.rem(d_me + offset + ndp, ndp)

    def q_copies(layer):
        return [
            pltpu.make_async_copy(qn_h.at[layer], qn.at[layer], sem_q.at[layer, 0]),
            pltpu.make_async_copy(go_h.at[layer], go.at[layer], sem_q.at[layer, 1]),
            pltpu.make_async_copy(qr_h.at[layer], qr.at[layer], sem_q.at[layer, 2]),
        ]

    def w_copies(layer, step):
        heads_of = pl.ds(step * HG, HG)
        return [
            pltpu.make_async_copy(wk_h.at[layer, heads_of], wk.at[layer, heads_of], sem_w.at[layer, step, 0]),
            pltpu.make_async_copy(wv_h.at[layer, heads_of], wv.at[layer, heads_of], sem_w.at[layer, step, 1]),
        ]

    own_rows = slice(MARGIN, MARGIN + tok)
    edge = MARGIN - tok
    k_copies = [
        pltpu.make_async_copy(lat_h, le.at[own_rows, :lat], sem_k.at[0]),
        pltpu.make_async_copy(kr_h, kr, sem_k.at[1]),
        pltpu.make_async_copy(hid_h, hid, sem_k.at[2]),
    ]
    for c in k_copies + q_copies(0) + w_copies(0, 0):
        c.start()

    barrier = pltpu.get_barrier_semaphore()

    def greet_cp(i):
        pl.semaphore_signal(barrier, inc=1, device_id=(cp_dev(i + 1), d_me), device_id_type=MESH)

    def greet_dp(i):
        pl.semaphore_signal(barrier, inc=1, device_id=(c_me, dp_dev(i + 1)), device_id_type=MESH)

    each(ncp - 1, greet_cp)
    each(ndp - 1, greet_dp)

    k_copies[0].wait()
    k_copies[1].wait()
    turned = kr[...].astype(F32)
    le[own_rows, lat:] = jnp.concatenate([turned, turned], axis=0).T.astype(BF)
    pl.semaphore_wait(barrier, ncp + ndp - 2)

    halo = [
        pltpu.make_async_remote_copy(
            le.at[own_rows], le.at[edge:MARGIN], sem_halo.at[0], sem_halo.at[1],
            device_id=(cp_dev(1), d_me), device_id_type=MESH,
        ),
        pltpu.make_async_remote_copy(
            le.at[MARGIN + tok - edge : MARGIN + tok], le.at[:edge], sem_halo.at[2], sem_halo.at[3],
            device_id=(cp_dev(2), d_me), device_id_type=MESH,
        ),
    ]
    for c in halo:
        c.start()

    k_copies[2].wait()
    width = hid.shape[1] // ncp
    rows_dev = width // ndp

    def turn(c):
        for j in range(width // 128):
            lanes = pl.ds(pl.multiple_of(c * width + j * 128, 128), 128)
            slab[j * 128 : j * 128 + 128, :] = hid[:, lanes].astype(F32).T
        pad = jnp.zeros((PIECE - rows_dev, tok), F32)
        for j in range(ndp):
            piece = jnp.concatenate([slab[j * rows_dev : (j + 1) * rows_dev, :], pad], axis=0)
            ht[j, pl.ds(pl.multiple_of(c * PIECE, PIECE), PIECE), :] = piece.astype(BF)

    each(ncp, turn)

    def my_lanes():
        return pl.ds(pl.multiple_of(d_me * tok, tok), tok)

    def hidden_copy(i):
        to = dp_dev(i + 1)
        return pltpu.make_async_remote_copy(
            ht.at[to], hr.at[:, my_lanes()], sem_hs.at[i], sem_hr.at[i],
            device_id=(c_me, to), device_id_type=MESH,
        )

    each(ndp - 1, lambda i: hidden_copy(i).start())
    hidden_own = pltpu.make_async_copy(ht.at[d_me], hr.at[:, my_lanes()], sem_own.at[0])
    hidden_own.start()

    acc[...] = jnp.zeros_like(acc)
    for s in range(2):
        t = c_me * tok + s * SUB + lax.broadcasted_iota(jnp.int32, (SUB, 128), 0)
        first = jnp.zeros((SUB, 128), jnp.int32)
        end = jnp.int32(0)
        for j in range(lens.shape[1]):
            end = end + lens[0, j]
            first = jnp.where(end <= t, end, first)
        for half in range(2):
            u = (
                c_me * tok - MARGIN + s * SUB + half * 128
                + lax.broadcasted_iota(jnp.int32, (SUB, 128), 1)
            )
            ok = (u >= first) & (u <= t)
            bias[s, :, half * 128 : half * 128 + 128] = jnp.where(ok, jnp.inf, -jnp.inf)
    low = lax.broadcasted_iota(jnp.int32, (SUB, 128), 1) < ROPE

    def out_parts(layer, half, to):
        tokens = pl.ds(pl.multiple_of(c_me * blk, blk), blk)
        return [
            (on.at[to, layer, half], dqn_h.at[layer, tokens, pl.ds(half * part_heads, part_heads)]),
            (orp.at[to, layer, half], dqr_h.at[layer, tokens, pl.ds(half * part_wide, part_wide)]),
        ]

    def out_copies(layer, half, i):
        to = cp_dev(i + 1)
        return [
            pltpu.make_async_remote_copy(
                src, dst, sem_os.at[layer, half, i, j], sem_or.at[layer, half, i, j],
                device_id=(to, d_me), device_id_type=MESH,
            )
            for j, (src, dst) in enumerate(out_parts(layer, half, to))
        ]

    def out_own(layer, half):
        return [
            pltpu.make_async_copy(src, dst, sem_oo.at[layer, half, j])
            for j, (src, dst) in enumerate(out_parts(layer, half, c_me))
        ]

    def widen(layer):
        for c in q_copies(layer):
            c.wait()

        def chunk(c):
            piece = pl.ds(pl.multiple_of(c * blk * heads, blk * heads), blk * heads)
            for wide_ref, ref in ((qf, qn), (gf, go)):
                value = ref[layer, piece, :].astype(F32)
                for t in range(blk):
                    at = pl.ds(c * (blk * PITCH) + t * PITCH, heads)
                    wide_ref[layer, at, :] = value[t * heads : (t + 1) * heads]

        each(tok // blk, chunk)

    def absorb(n, slot, i):
        layer, step = n // steps, lax.rem(n, steps)
        h = step * HG + i
        a = dot(qf[layer, pl.ds(h, tok, stride=PITCH), :].astype(BF), wk[layer, h], 1, 0).astype(BF)
        b = dot(gf[layer, pl.ds(h, tok, stride=PITCH), :].astype(BF), wv[layer, h], 1, 1).astype(BF)
        lanes = pl.ds(pl.multiple_of((step * (HG // 2) + i // 2) * 128, 128), 128)
        mine = slice(i * SUB, i * SUB + SUB)
        for s in range(2):
            sub = slice(s * SUB, s * SUB + SUB)
            ql[slot, s, mine, :lat] = a[sub]
            gl[slot, s, mine, :] = b[sub]
            pair = qr[layer, sub, lanes].astype(F32)
            pair = jnp.where(low if i % 2 == 0 else ~low, pair, 0.0)
            ql[slot, s, mine, lat:] = pair.astype(BF)

    def scores(slot, s):
        win = slice(s * SUB, s * SUB + WIN)
        return dot(ql[slot, s], le[win, :], 1, 1), dot(gl[slot, s], le[win, :lat], 1, 1)

    def softmax(s, score, dprob, j):
        part_of = slice(j * 2 * SUB, (j + 1) * 2 * SUB)
        x = jnp.minimum(score[part_of].reshape(2, SUB, WIN), bias[s][None]).reshape(2 * SUB, WIN)
        e = jnp.exp((x - jnp.max(x, axis=1, keepdims=True)) * scale)
        d = dprob[part_of]
        inv = 1.0 / jnp.sum(e, axis=1, keepdims=True)
        delta = jnp.sum(e * d, axis=1, keepdims=True) * inv
        return (e * (inv * scale) * (d - delta)).astype(BF), (e * inv).astype(BF)

    def add_keys(slot, s, ds, low_p):
        win = slice(s * SUB, s * SUB + WIN)
        acc[win, :] += dot(ds, ql[slot, s], 0, 0)
        acc[win, :lat] += dot(low_p, gl[slot, s], 0, 0)

    def query_side(step, s, ds):
        win = slice(s * SUB, s * SUB + WIN)
        d = dot(ds, le[win, :], 1, 0)
        for i in range(HG):
            dq[i, s * SUB : s * SUB + SUB, :] = d[i * SUB : i * SUB + SUB, :lat].astype(BF)
        for j in range(HG // 2):
            even = d[2 * j * SUB : (2 * j + 1) * SUB, lat:]
            odd = d[(2 * j + 1) * SUB : (2 * j + 2) * SUB, lat:]
            both = jnp.where(low, even, odd).astype(BF)
            lanes = pl.ds(pl.multiple_of((lax.rem(step, 2) * (HG // 2) + j) * 128, 128), 128)
            for q in range(SUB // blk):
                ro[s * (SUB // blk) + q, :, lanes] = both[q * blk : q * blk + blk]

    def query_out(layer, step):
        for i in range(HG):
            back_q = dot(dq[i], wk[layer, step * HG + i], 1, 1)
            for q in range(ncp):
                of[q, pl.ds(lax.rem(step, 2) * HG + i, blk, stride=OUT_PITCH), :] = back_q[q * blk : q * blk + blk]

    def send_out(layer, half):
        def place(k):
            b = plan[0, c_me, k]
            for t in range(blk):
                on[k, layer, half, t] = of[b, t * OUT_PITCH : t * OUT_PITCH + part_heads, :].astype(BF)
            orp[k, layer, half] = ro[b]

        each(ncp, place)

        def start(i):
            for c in out_copies(layer, half, i):
                c.start()

        each(ncp - 1, start)
        for c in out_own(layer, half):
            c.start()

    def step_body(n, layer, defer, more):
        slot = lax.rem(n, 2)
        follow = n + 1
        step = n - layer * steps
        if not defer:

            @pl.when(step == 1)
            def _():
                widen(layer + 1)

        if more:
            ahead = n + 3

            @pl.when(ahead < layers * steps)
            def _():
                for c in w_copies(ahead // steps, lax.rem(ahead, steps)):
                    c.start()

            for c in w_copies(follow // steps, lax.rem(follow, steps)):
                c.wait()

        pend = None
        for s in range(2):
            score, dprob = scores(slot, s)
            if pend is not None:
                add_keys(slot, *pend)
                if not defer:
                    query_side(step, pend[0], pend[1])
            ds, low_p = [], []
            for j in range(HG // 2):
                x, p = softmax(s, score, dprob, j)
                ds.append(x)
                low_p.append(p)
                if more and s == 0:
                    absorb(follow, 1 - slot, 2 * j)
                    absorb(follow, 1 - slot, 2 * j + 1)
            ds = jnp.concatenate(ds, axis=0)
            low_p = jnp.concatenate(low_p, axis=0)
            if defer:
                kept[step, s] = ds
            pend = (s, ds, low_p)
        add_keys(slot, *pend)
        if not defer:
            query_side(step, pend[0], pend[1])
            query_out(layer, step)

            @pl.when(lax.rem(step, 2) == 1)
            def _():
                send_out(layer, step // 2)

    back_copies = [
        pltpu.make_async_remote_copy(
            back.at[edge:MARGIN], back1, sem_back.at[0], sem_back.at[1],
            device_id=(cp_dev(-1), d_me), device_id_type=MESH,
        ),
        pltpu.make_async_remote_copy(
            back.at[:edge], back2, sem_back.at[2], sem_back.at[3],
            device_id=(cp_dev(-2), d_me), device_id_type=MESH,
        ),
    ]

    widen(0)
    for c in w_copies(0, 1):
        c.start()
    for c in w_copies(0, 0):
        c.wait()
    for c in q_copies(1) + w_copies(0, 2):
        c.start()
    for i in range(HG):
        absorb(jnp.int32(0), 0, i)
    for c in halo:
        c.wait_recv()

    last = layers - 1
    each(last * steps, lambda n: step_body(n, n // steps, False, True))
    each(steps - 1, lambda n: step_body(n + last * steps, last, True, True))
    step_body(jnp.int32(layers * steps - 1), last, True, False)
    back[...] = acc[:MARGIN, :].astype(BF)
    for c in back_copies:
        c.start()

    def late_queries(step):
        for s in range(2):
            query_side(step, s, kept[step, s])
        query_out(last, step)

    each(2, late_queries)
    send_out(last, 0)

    for c in back_copies:
        c.wait_recv()
    total = acc[own_rows, :] + back1[...].astype(F32)
    late = total[tok - edge :] + back2[...].astype(F32)
    total = jnp.concatenate([total[: tok - edge], late], axis=0)
    rope = total[:, lat:]
    rope = rope + pltpu.roll(rope, ROPE, 1)
    low_all = lax.broadcasted_iota(jnp.int32, (tok, 128), 1) < ROPE
    rope = jnp.where(low_all, rope, 0.0)
    half = tok // 2
    quarter = half // 2
    for w in range(2):
        of_half = slice(w * half, w * half + half)
        ja[of_half, :] = total[of_half, :FIRST].astype(BF)
        jb[w, :half, :] = total[of_half, FIRST:lat].astype(BF)
        top = rope[w * half : w * half + quarter]
        bottom = pltpu.roll(rope[w * half + quarter : (w + 1) * half], ROPE, 1)
        jb[w, half:, :] = (top + bottom).astype(BF)
    dlat[...] = total[:, :lat].astype(BF)
    dkr[...] = rope.T[:ROPE].astype(BF)

    y, z = d_me // side, lax.rem(d_me, side)
    other = ndp // side

    def place_of(yy, zz, which, ch):
        if ch == 1:
            return gb.at[yy * side + zz, which]
        return ga.at[pl.ds(pl.multiple_of((yy * side + zz) * tok + which * half, half), half)]

    def mine_of(which, ch):
        return jb.at[which] if ch == 1 else ja.at[which * half : which * half + half]

    def ring(value, offset, n):
        return lax.rem(value + offset + n, n)

    def near(ch, which, k):
        src = mine_of(which, ch)
        to = y * side + ring(z, k, side) if which == 0 else ring(y, k, other) * side + z
        return pltpu.make_async_remote_copy(
            src, place_of(y, z, which, ch), sem_near.at[ch, which, 0, k - 1], sem_near.at[ch, which, 1, k - 1],
            device_id=(c_me, to), device_id_type=MESH,
        )

    def forward(ch, which, j, k):
        if which == 0:
            ref = place_of(y, ring(z, -j, side), 0, ch)
            to = ring(y, k, other) * side + z
        else:
            ref = place_of(ring(y, -j, other), z, 1, ch)
            to = y * side + ring(z, k, side)
        src = mine_of(which, ch) if j == 0 else ref
        return pltpu.make_async_remote_copy(
            src, ref, sem_fwd_s.at[ch, which, j, k - 1], sem_fwd_r.at[ch, which, j, k - 1],
            device_id=(c_me, to), device_id_type=MESH,
        )

    def relay(which, j, back_by):
        step = 1 if back_by == 0 else -1
        if which == 0:
            ref = place_of(ring(y, -step, other), ring(z, -j, side), 0, 0)
            to = ring(y, step, other) * side + z
        else:
            ref = place_of(ring(y, -j, other), ring(z, -step, side), 1, 0)
            to = y * side + ring(z, step, side)
        ref = ref.at[pl.ds(back_by * quarter, quarter)]
        return pltpu.make_async_remote_copy(
            ref, ref, sem_rel.at[which, j, back_by, 0], sem_rel.at[which, j, back_by, 1],
            device_id=(c_me, to), device_id_type=MESH,
        )

    for ch in range(2):
        for k in (1, 3, 2):
            near(ch, 0, k).start()
            near(ch, 1, k).start()
        for k in (1, 3) if ch == 0 else (1, 3, 2):
            forward(ch, 0, 0, k).start()
            forward(ch, 1, 0, k).start()
    gather_own = [
        pltpu.make_async_copy(ja, ga.at[pl.ds(pl.multiple_of(d_me * tok, tok), tok)], sem_own.at[0]),
        pltpu.make_async_copy(jb, gb.at[d_me], sem_own.at[1]),
    ]
    hidden_own.wait()
    for c in gather_own:
        c.start()
    each(2, lambda i: late_queries(i + 2))
    send_out(last, 1)
    for j in (1, 3, 2):
        for which in range(2):
            near(0, which, j).wait_recv()
            for k in (1, 3):
                forward(0, which, j, k).start()
    for j in (0, 1, 3, 2):
        for which in range(2):
            for k in (1, 3):
                forward(0, which, j, k).wait_recv()
                relay(which, j, k // 2).start()
    for j in (1, 3, 2):
        for which in range(2):
            near(1, which, j).wait_recv()
            for k in (1, 3, 2):
                forward(1, which, j, k).start()
    each(ndp - 1, lambda i: hidden_copy(i).wait())
    for c in gather_own:
        c.wait()
    for j in (0, 1, 3, 2):
        for which in range(2):
            for back_by in range(2):
                relay(which, j, back_by).wait_recv()

    def part_copy(ch, i):
        to = cp_dev(i + 1)
        src, dst = ((pa, ra), (pb, rb))[ch]
        return pltpu.make_async_remote_copy(
            src.at[to], dst.at[i], sem_ps.at[ch, i], sem_pr.at[ch, i],
            device_id=(to, d_me), device_id_type=MESH,
        )

    block = 4 * PIECE

    def product(c):
        d = dot(hr[pl.ds(pl.multiple_of(c * block, block), block), :], ga[...], 1, 0).astype(BF)
        for i in range(4):
            pa[c * 4 + i] = d[i * PIECE : (i + 1) * PIECE]

    each(ncp // 4, product)
    each(ncp - 1, lambda i: part_copy(0, i).start())
    for j in range(4):
        for which in range(2):
            for k in (1, 2, 3):
                forward(1, which, j, k).wait_recv()

    def unfold(i):
        for w in range(2):
            at = i * tok + w * half
            gc[pl.ds(pl.multiple_of(at, half), half), :128] = gb[i, w, :half, :]
            folded = gb[i, w, half:, :].astype(F32)
            gc[pl.ds(pl.multiple_of(at, quarter), quarter), 128:] = folded.astype(BF)
            gc[pl.ds(pl.multiple_of(at + quarter, quarter), quarter), 128:] = pltpu.roll(folded, ROPE, 1).astype(BF)

    each(ndp, unfold)

    def product_rest(c):
        d = dot(hr[pl.ds(pl.multiple_of(c * block, block), block), :], gc[...], 1, 0)
        for i in range(4):
            piece = d[i * PIECE : (i + 1) * PIECE]
            pb[c * 4 + i, :PIECE, :] = piece[:, :128].astype(BF)
            folded = jnp.where(low[: PIECE // 2], piece[: PIECE // 2, 128:], pltpu.roll(piece[PIECE // 2 :, 128:], ROPE, 1))
            pb[c * 4 + i, PIECE:, :] = folded.astype(BF)

    each(ncp // 4, product_rest)
    each(ncp - 1, lambda i: part_copy(1, i).start())
    for c in halo + back_copies:
        c.wait_send()
    for which in range(2):
        for ch in range(2):
            for k in (1, 2, 3):
                near(ch, which, k).wait_send()
            for j in range(4):
                for k in (1, 3) if ch == 0 else (1, 2, 3):
                    forward(ch, which, j, k).wait_send()
        for j in range(4):
            for back_by in range(2):
                relay(which, j, back_by).wait_send()
    first = pa[c_me].astype(F32)
    for i in range(ncp - 1):
        part_copy(0, i).wait_recv()
        first = first + ra[i].astype(F32)
    dw[:, :FIRST] = first[:rows_dev]
    rest = pb[c_me].astype(F32)
    for i in range(ncp - 1):
        part_copy(1, i).wait_recv()
        rest = rest + rb[i].astype(F32)
    dw[:, FIRST:lat] = rest[:rows_dev]
    dw[: PIECE // 2, lat:] = rest[PIECE:, :ROPE]
    dw[PIECE // 2 :, lat:] = pltpu.roll(rest[PIECE:], ROPE, 1)[: rows_dev - PIECE // 2, :ROPE]

    for ch in range(2):
        each(ncp - 1, lambda i: part_copy(ch, i).wait_send())

    def finish(n):
        layer, half = n // 2, lax.rem(n, 2)
        for c in out_own(layer, half):
            c.wait()

        def one(i):
            for c in out_copies(layer, half, i):
                c.wait()

        each(ncp - 1, one)

    each(2 * layers, finish)


def pass_on(*refs):
    count = (len(refs) - 2) // 3
    came, went = refs[-2:]
    moves = []
    for i in range(count):
        src, dst, held = refs[i], refs[count + i], refs[2 * count + i]
        pieces = [(0, slice(None))]
        if len(src.shape) > 2:
            cut = src.shape[1] // 4
            pieces = [(n, (n // 4, slice(n % 4 * cut, (n % 4 + 1) * cut))) for n in range(4 * src.shape[0])]
        for n, at in pieces:
            moves.append(
                (
                    pltpu.make_async_copy(src.at[at], held.at[at], came.at[i, n]),
                    pltpu.make_async_copy(held.at[at], dst.at[at], went.at[i, n]),
                )
            )
    for load, _ in moves:
        load.start()
    for load, store in moves:
        load.wait()
        store.start()
    for _, store in moves:
        store.wait()


def on_device(q_nope, q_rope, grad_out, latent, key_rope, hidden_in, w_uk, w_uv, doc_lengths, plan):
    ncp = lax.axis_size("cp")
    ndp = lax.axis_size("dp")
    side = math.isqrt(ndp)
    layers, _, tok, heads, head = q_nope.shape
    wide = q_rope.shape[3]
    lat = latent.shape[2]
    model = hidden_in.shape[2]
    ext = lat + 2 * ROPE
    rows = tok * heads
    smem = pl.BlockSpec(memory_space=pltpu.SMEM)
    hbm = pl.BlockSpec(memory_space=pl.ANY)
    vmem = pl.BlockSpec(memory_space=pltpu.VMEM)
    dma = pltpu.SemaphoreType.DMA
    results = pl.pallas_call(
        functools.partial(kernel, ncp, ndp, side),
        out_shape=(
            jax.ShapeDtypeStruct((layers, tok, heads, head), BF),
            jax.ShapeDtypeStruct((layers, tok, wide), BF),
            jax.ShapeDtypeStruct((tok, lat), BF),
            jax.ShapeDtypeStruct((ROPE, tok), BF),
            jax.ShapeDtypeStruct((model // (ncp * ndp), lat + ROPE), F32),
        ),
        in_specs=[smem, smem] + [hbm] * 8,
        out_specs=(hbm, hbm, vmem, vmem, vmem),
        scratch_shapes=[
            pltpu.VMEM((layers, rows, head), BF),
            pltpu.VMEM((layers, tok, wide), BF),
            pltpu.VMEM((layers, rows, head), BF),
            pltpu.VMEM((MARGIN + tok, ext), BF),
            pltpu.VMEM((ROPE, tok), BF),
            pltpu.VMEM((tok, model), BF),
            pltpu.VMEM(w_uk.shape, BF),
            pltpu.VMEM(w_uv.shape, BF),
            pltpu.VMEM((layers, tok * PITCH, head), F32),
            pltpu.VMEM((layers, tok * PITCH, head), F32),
            pltpu.VMEM((ncp, tok // ncp * OUT_PITCH, head), F32),
            pltpu.VMEM((ncp, tok // ncp, wide // 2), BF),
            pltpu.VMEM((2, 2, HG * SUB, ext), BF),
            pltpu.VMEM((2, 2, HG * SUB, lat), BF),
            pltpu.VMEM((HG, tok, lat), BF),
            pltpu.VMEM((heads // HG, 2, HG * SUB, WIN), BF),
            pltpu.VMEM((2, SUB, WIN), F32),
            pltpu.VMEM((MARGIN + tok, ext), F32),
            pltpu.VMEM((ncp, layers, 2, tok // ncp, heads // 2, head), BF),
            pltpu.VMEM((ncp, layers, 2, tok // ncp, wide // 2), BF),
            pltpu.VMEM((model // ncp, tok), F32),
            pltpu.VMEM((ndp, ncp * PIECE, tok), BF),
            pltpu.VMEM((ncp * PIECE, ndp * tok), BF),
            pltpu.VMEM((MARGIN, ext), BF),
            pltpu.VMEM((tok, ext), BF),
            pltpu.VMEM((MARGIN - tok, ext), BF),
            pltpu.VMEM((tok, FIRST), BF),
            pltpu.VMEM((2, tok // 2 + tok // 4, 128), BF),
            pltpu.VMEM((ndp * tok, FIRST), BF),
            pltpu.VMEM((ndp, 2, tok // 2 + tok // 4, 128), BF),
            pltpu.VMEM((ndp * tok, 256), BF),
            pltpu.VMEM((ncp, PIECE, FIRST), BF),
            pltpu.VMEM((ncp, PIECE + PIECE // 2, 128), BF),
            pltpu.VMEM((ncp - 1, PIECE, FIRST), BF),
            pltpu.VMEM((ncp - 1, PIECE + PIECE // 2, 128), BF),
            dma((layers, 3)),
            dma((layers, heads // HG, 2)),
            dma((3,)),
            dma((4,)),
            dma((ndp - 1,)),
            dma((ndp - 1,)),
            dma((layers, 2, ncp - 1, 2)),
            dma((layers, 2, ncp - 1, 2)),
            dma((layers, 2, 2)),
            dma((4,)),
            dma((2, 2, 2, 3)),
            dma((2, 2, 4, 3)),
            dma((2, 2, 4, 3)),
            dma((2, 4, 2, 2)),
            dma((2, ncp - 1)),
            dma((2, ncp - 1)),
            dma((2,)),
        ],
        compiler_params=pltpu.CompilerParams(
            collective_id=0, has_side_effects=True, vmem_limit_bytes=60 * 1024 * 1024
        ),
        name="attention_backward",
    )(
        doc_lengths,
        plan,
        q_nope.reshape(layers, rows, head),
        q_rope[:, 0],
        grad_out.reshape(layers, rows, head),
        latent[0],
        key_rope[0],
        hidden_in[0],
        w_uk,
        w_uv,
    )
    dqn, dqr, dlat, dkr, dw = pl.pallas_call(
        pass_on,
        out_shape=tuple(jax.ShapeDtypeStruct(r.shape, r.dtype) for r in results),
        in_specs=[hbm] * 5,
        out_specs=(hbm,) * 5,
        scratch_shapes=[pltpu.VMEM(r.shape, r.dtype) for r in results] + [dma((5, 8)), dma((5, 8))],
        name="pass_on",
    )(*results)
    return (
        dqn.reshape(q_nope.shape),
        dqr.reshape(q_rope.shape),
        dlat[None],
        dkr[None],
        dw,
    )


def solution(mesh):
    placed = (
        P(None, "dp", "cp", None, None),
        P(None, "dp", "cp", None),
        P(None, "dp", "cp", None, None),
        P("dp", "cp", None),
        P("dp", None, "cp"),
        P("dp", "cp", None),
        P(),
        P(),
        P("dp", None),
        P("dp", None, None),
    )
    return jax.shard_map(
        on_device,
        mesh=mesh,
        in_specs=placed,
        out_specs=(
            P(None, "dp", "cp", None, None),
            P(None, "dp", "cp", None),
            P("dp", "cp", None),
            P("dp", None, "cp"),
            P(("cp", "dp"), None),
        ),
        check_vma=False,
    )
```

```python
import functools
import math

import jax
import jax.numpy as jnp
from jax import lax
from jax.experimental import pallas as pl
from jax.experimental.pallas import tpu as pltpu
from jax.sharding import PartitionSpec as P

BF = jnp.bfloat16
F32 = jnp.float32
MESH = pl.DeviceIdType.MESH
MARGIN = 192
SUB = 64
WIN = 256
HG = 8
PITCH = 36
OUT_PITCH = 20
ROPE = 64
FIRST = 384
PIECE = 64


def dot(a, b, ca, cb):
    return lax.dot_general(a, b, (((ca,), (cb,)), ((), ())), preferred_element_type=F32)


def each(count, body):
    def step(i, carry):
        body(i)
        return carry

    lax.fori_loop(0, count, step, 0)


def kernel(
    ncp, ndp, side,
    lens, plan, qn_h, qr_h, go_h, lat_h, kr_h, hid_h, wk_h, wv_h,
    dqn_h, dqr_h, dlat, dkr, dw,
    qn, qr, go, le, kr, hid, wk, wv, qf, gf, of, ro, ql, gl, dq, kept, bias, acc, on, orp,
    slab, ht, hr, back, back1, back2, ja, jb, ga, gb, gc, pa, pb, ra, rb,
    sem_q, sem_w, sem_k, sem_halo, sem_hs, sem_hr, sem_os, sem_or, sem_oo, sem_back,
    sem_near, sem_fwd_s, sem_fwd_r, sem_rel, sem_ps, sem_pr, sem_own,
):
    layers, rows, head = qn.shape
    tok = qr.shape[1]
    heads = rows // tok
    lat = gl.shape[3]
    ext = le.shape[1]
    steps = heads // HG
    blk = tok // ncp
    part_heads = heads // 2
    part_wide = part_heads * ROPE
    scale = 1.0 / math.sqrt(head + ROPE)
    c_me = lax.axis_index("cp")
    d_me = lax.axis_index("dp")

    def cp_dev(offset):
        return lax.rem(c_me + offset + ncp, ncp)

    def dp_dev(offset):
        return lax.rem(d_me + offset + ndp, ndp)

    def q_copies(layer):
        return [
            pltpu.make_async_copy(qn_h.at[layer], qn.at[layer], sem_q.at[layer, 0]),
            pltpu.make_async_copy(go_h.at[layer], go.at[layer], sem_q.at[layer, 1]),
            pltpu.make_async_copy(qr_h.at[layer], qr.at[layer], sem_q.at[layer, 2]),
        ]

    def w_copies(layer, step):
        heads_of = pl.ds(step * HG, HG)
        return [
            pltpu.make_async_copy(wk_h.at[layer, heads_of], wk.at[layer, heads_of], sem_w.at[layer, step, 0]),
            pltpu.make_async_copy(wv_h.at[layer, heads_of], wv.at[layer, heads_of], sem_w.at[layer, step, 1]),
        ]

    own_rows = slice(MARGIN, MARGIN + tok)
    edge = MARGIN - tok
    k_copies = [
        pltpu.make_async_copy(lat_h, le.at[own_rows, :lat], sem_k.at[0]),
        pltpu.make_async_copy(kr_h, kr, sem_k.at[1]),
        pltpu.make_async_copy(hid_h, hid, sem_k.at[2]),
    ]
    for c in k_copies + q_copies(0) + w_copies(0, 0):
        c.start()

    barrier = pltpu.get_barrier_semaphore()

    def greet_cp(i):
        pl.semaphore_signal(barrier, inc=1, device_id=(cp_dev(i + 1), d_me), device_id_type=MESH)

    def greet_dp(i):
        pl.semaphore_signal(barrier, inc=1, device_id=(c_me, dp_dev(i + 1)), device_id_type=MESH)

    each(ncp - 1, greet_cp)
    each(ndp - 1, greet_dp)

    k_copies[0].wait()
    k_copies[1].wait()
    turned = kr[...].astype(F32)
    le[own_rows, lat:] = jnp.concatenate([turned, turned], axis=0).T.astype(BF)
    pl.semaphore_wait(barrier, ncp + ndp - 2)

    halo = [
        pltpu.make_async_remote_copy(
            le.at[own_rows], le.at[edge:MARGIN], sem_halo.at[0], sem_halo.at[1],
            device_id=(cp_dev(1), d_me), device_id_type=MESH,
        ),
        pltpu.make_async_remote_copy(
            le.at[MARGIN + tok - edge : MARGIN + tok], le.at[:edge], sem_halo.at[2], sem_halo.at[3],
            device_id=(cp_dev(2), d_me), device_id_type=MESH,
        ),
    ]
    for c in halo:
        c.start()

    k_copies[2].wait()
    width = hid.shape[1] // ncp
    rows_dev = width // ndp

    def turn(c):
        for j in range(width // 128):
            lanes = pl.ds(pl.multiple_of(c * width + j * 128, 128), 128)
            slab[j * 128 : j * 128 + 128, :] = hid[:, lanes].astype(F32).T
        pad = jnp.zeros((PIECE - rows_dev, tok), F32)
        for j in range(ndp):
            piece = jnp.concatenate([slab[j * rows_dev : (j + 1) * rows_dev, :], pad], axis=0)
            ht[j, pl.ds(pl.multiple_of(c * PIECE, PIECE), PIECE), :] = piece.astype(BF)

    each(ncp, turn)

    def my_lanes():
        return pl.ds(pl.multiple_of(d_me * tok, tok), tok)

    def hidden_copy(i):
        to = dp_dev(i + 1)
        return pltpu.make_async_remote_copy(
            ht.at[to], hr.at[:, my_lanes()], sem_hs.at[i], sem_hr.at[i],
            device_id=(c_me, to), device_id_type=MESH,
        )

    each(ndp - 1, lambda i: hidden_copy(i).start())
    hidden_own = pltpu.make_async_copy(ht.at[d_me], hr.at[:, my_lanes()], sem_own.at[0])
    hidden_own.start()

    acc[...] = jnp.zeros_like(acc)
    for s in range(2):
        t = c_me * tok + s * SUB + lax.broadcasted_iota(jnp.int32, (SUB, 128), 0)
        first = jnp.zeros((SUB, 128), jnp.int32)
        end = jnp.int32(0)
        for j in range(lens.shape[1]):
            end = end + lens[0, j]
            first = jnp.where(end <= t, end, first)
        for half in range(2):
            u = (
                c_me * tok - MARGIN + s * SUB + half * 128
                + lax.broadcasted_iota(jnp.int32, (SUB, 128), 1)
            )
            ok = (u >= first) & (u <= t)
            bias[s, :, half * 128 : half * 128 + 128] = jnp.where(ok, jnp.inf, -jnp.inf)
    low = lax.broadcasted_iota(jnp.int32, (SUB, 128), 1) < ROPE

    def out_parts(layer, half, to):
        tokens = pl.ds(pl.multiple_of(c_me * blk, blk), blk)
        return [
            (on.at[to, layer, half], dqn_h.at[layer, tokens, pl.ds(half * part_heads, part_heads)]),
            (orp.at[to, layer, half], dqr_h.at[layer, tokens, pl.ds(half * part_wide, part_wide)]),
        ]

    def out_copies(layer, half, i):
        to = cp_dev(i + 1)
        return [
            pltpu.make_async_remote_copy(
                src, dst, sem_os.at[layer, half, i, j], sem_or.at[layer, half, i, j],
                device_id=(to, d_me), device_id_type=MESH,
            )
            for j, (src, dst) in enumerate(out_parts(layer, half, to))
        ]

    def out_own(layer, half):
        return [
            pltpu.make_async_copy(src, dst, sem_oo.at[layer, half, j])
            for j, (src, dst) in enumerate(out_parts(layer, half, c_me))
        ]

    def widen(layer):
        for c in q_copies(layer):
            c.wait()

        def chunk(c):
            piece = pl.ds(pl.multiple_of(c * blk * heads, blk * heads), blk * heads)
            for wide_ref, ref in ((qf, qn), (gf, go)):
                value = ref[layer, piece, :].astype(F32)
                for t in range(blk):
                    at = pl.ds(c * (blk * PITCH) + t * PITCH, heads)
                    wide_ref[layer, at, :] = value[t * heads : (t + 1) * heads]

        each(tok // blk, chunk)

    def absorb(n, slot, i):
        layer, step = n // steps, lax.rem(n, steps)
        h = step * HG + i
        a = dot(qf[layer, pl.ds(h, tok, stride=PITCH), :].astype(BF), wk[layer, h], 1, 0).astype(BF)
        b = dot(gf[layer, pl.ds(h, tok, stride=PITCH), :].astype(BF), wv[layer, h], 1, 1).astype(BF)
        lanes = pl.ds(pl.multiple_of((step * (HG // 2) + i // 2) * 128, 128), 128)
        mine = slice(i * SUB, i * SUB + SUB)
        for s in range(2):
            sub = slice(s * SUB, s * SUB + SUB)
            ql[slot, s, mine, :lat] = a[sub]
            gl[slot, s, mine, :] = b[sub]
            pair = qr[layer, sub, lanes].astype(F32)
            pair = jnp.where(low if i % 2 == 0 else ~low, pair, 0.0)
            ql[slot, s, mine, lat:] = pair.astype(BF)

    def scores(slot, s):
        win = slice(s * SUB, s * SUB + WIN)
        return dot(ql[slot, s], le[win, :], 1, 1), dot(gl[slot, s], le[win, :lat], 1, 1)

    def softmax(s, score, dprob, j):
        part_of = slice(j * 2 * SUB, (j + 1) * 2 * SUB)
        x = jnp.minimum(score[part_of].reshape(2, SUB, WIN), bias[s][None]).reshape(2 * SUB, WIN)
        e = jnp.exp((x - jnp.max(x, axis=1, keepdims=True)) * scale)
        d = dprob[part_of]
        inv = 1.0 / jnp.sum(e, axis=1, keepdims=True)
        delta = jnp.sum(e * d, axis=1, keepdims=True) * inv
        return (e * (inv * scale) * (d - delta)).astype(BF), (e * inv).astype(BF)

    def add_keys(slot, s, ds, low_p):
        win = slice(s * SUB, s * SUB + WIN)
        acc[win, :] += dot(ds, ql[slot, s], 0, 0)
        acc[win, :lat] += dot(low_p, gl[slot, s], 0, 0)

    def query_side(step, s, ds):
        win = slice(s * SUB, s * SUB + WIN)
        d = dot(ds, le[win, :], 1, 0)
        for i in range(HG):
            dq[i, s * SUB : s * SUB + SUB, :] = d[i * SUB : i * SUB + SUB, :lat].astype(BF)
        for j in range(HG // 2):
            even = d[2 * j * SUB : (2 * j + 1) * SUB, lat:]
            odd = d[(2 * j + 1) * SUB : (2 * j + 2) * SUB, lat:]
            both = jnp.where(low, even, odd).astype(BF)
            lanes = pl.ds(pl.multiple_of((lax.rem(step, 2) * (HG // 2) + j) * 128, 128), 128)
            for q in range(SUB // blk):
                ro[s * (SUB // blk) + q, :, lanes] = both[q * blk : q * blk + blk]

    def query_out(layer, step):
        for i in range(HG):
            back_q = dot(dq[i], wk[layer, step * HG + i], 1, 1)
            for q in range(ncp):
                of[q, pl.ds(lax.rem(step, 2) * HG + i, blk, stride=OUT_PITCH), :] = back_q[q * blk : q * blk + blk]

    def send_out(layer, half):
        def place(k):
            b = plan[0, c_me, k]
            for t in range(blk):
                on[k, layer, half, t] = of[b, t * OUT_PITCH : t * OUT_PITCH + part_heads, :].astype(BF)
            orp[k, layer, half] = ro[b]

        each(ncp, place)

        def start(i):
            for c in out_copies(layer, half, i):
                c.start()

        each(ncp - 1, start)
        for c in out_own(layer, half):
            c.start()

    def step_body(n, layer, defer, more):
        slot = lax.rem(n, 2)
        follow = n + 1
        step = n - layer * steps
        if not defer:

            @pl.when(step == 1)
            def _():
                widen(layer + 1)

        if more:
            ahead = n + 3

            @pl.when(ahead < layers * steps)
            def _():
                for c in w_copies(ahead // steps, lax.rem(ahead, steps)):
                    c.start()

            for c in w_copies(follow // steps, lax.rem(follow, steps)):
                c.wait()

        pend = None
        for s in range(2):
            score, dprob = scores(slot, s)
            if pend is not None:
                add_keys(slot, *pend)
                if not defer:
                    query_side(step, pend[0], pend[1])
            ds, low_p = [], []
            for j in range(HG // 2):
                x, p = softmax(s, score, dprob, j)
                ds.append(x)
                low_p.append(p)
                if more and s == 0:
                    absorb(follow, 1 - slot, 2 * j)
                    absorb(follow, 1 - slot, 2 * j + 1)
            ds = jnp.concatenate(ds, axis=0)
            low_p = jnp.concatenate(low_p, axis=0)
            if defer:
                kept[step, s] = ds
            pend = (s, ds, low_p)
        add_keys(slot, *pend)
        if not defer:
            query_side(step, pend[0], pend[1])
            query_out(layer, step)

            @pl.when(lax.rem(step, 2) == 1)
            def _():
                send_out(layer, step // 2)

    back_copies = [
        pltpu.make_async_remote_copy(
            back.at[edge:MARGIN], back1, sem_back.at[0], sem_back.at[1],
            device_id=(cp_dev(-1), d_me), device_id_type=MESH,
        ),
        pltpu.make_async_remote_copy(
            back.at[:edge], back2, sem_back.at[2], sem_back.at[3],
            device_id=(cp_dev(-2), d_me), device_id_type=MESH,
        ),
    ]

    widen(0)
    for c in w_copies(0, 1):
        c.start()
    for c in w_copies(0, 0):
        c.wait()
    for c in q_copies(1) + w_copies(0, 2):
        c.start()
    for i in range(HG):
        absorb(jnp.int32(0), 0, i)
    for c in halo:
        c.wait_recv()

    last = layers - 1
    each(last * steps, lambda n: step_body(n, n // steps, False, True))
    each(steps - 1, lambda n: step_body(n + last * steps, last, True, True))
    step_body(jnp.int32(layers * steps - 1), last, True, False)
    back[...] = acc[:MARGIN, :].astype(BF)
    for c in back_copies:
        c.start()

    def late_queries(step):
        for s in range(2):
            query_side(step, s, kept[step, s])
        query_out(last, step)

    each(2, late_queries)
    send_out(last, 0)

    for c in back_copies:
        c.wait_recv()
    total = acc[own_rows, :] + back1[...].astype(F32)
    late = total[tok - edge :] + back2[...].astype(F32)
    total = jnp.concatenate([total[: tok - edge], late], axis=0)
    rope = total[:, lat:]
    rope = rope + pltpu.roll(rope, ROPE, 1)
    low_all = lax.broadcasted_iota(jnp.int32, (tok, 128), 1) < ROPE
    rope = jnp.where(low_all, rope, 0.0)
    half = tok // 2
    quarter = half // 2
    for w in range(2):
        of_half = slice(w * half, w * half + half)
        ja[of_half, :] = total[of_half, :FIRST].astype(BF)
        jb[w, :half, :] = total[of_half, FIRST:lat].astype(BF)
        top = rope[w * half : w * half + quarter]
        bottom = pltpu.roll(rope[w * half + quarter : (w + 1) * half], ROPE, 1)
        jb[w, half:, :] = (top + bottom).astype(BF)
    dlat[...] = total[:, :lat].astype(BF)
    dkr[...] = rope.T[:ROPE].astype(BF)

    y, z = d_me // side, lax.rem(d_me, side)
    other = ndp // side

    def place_of(yy, zz, which, ch):
        if ch == 1:
            return gb.at[yy * side + zz, which]
        return ga.at[pl.ds(pl.multiple_of((yy * side + zz) * tok + which * half, half), half)]

    def mine_of(which, ch):
        return jb.at[which] if ch == 1 else ja.at[which * half : which * half + half]

    def ring(value, offset, n):
        return lax.rem(value + offset + n, n)

    def near(ch, which, k):
        src = mine_of(which, ch)
        to = y * side + ring(z, k, side) if which == 0 else ring(y, k, other) * side + z
        return pltpu.make_async_remote_copy(
            src, place_of(y, z, which, ch), sem_near.at[ch, which, 0, k - 1], sem_near.at[ch, which, 1, k - 1],
            device_id=(c_me, to), device_id_type=MESH,
        )

    def forward(ch, which, j, k):
        if which == 0:
            ref = place_of(y, ring(z, -j, side), 0, ch)
            to = ring(y, k, other) * side + z
        else:
            ref = place_of(ring(y, -j, other), z, 1, ch)
            to = y * side + ring(z, k, side)
        src = mine_of(which, ch) if j == 0 else ref
        return pltpu.make_async_remote_copy(
            src, ref, sem_fwd_s.at[ch, which, j, k - 1], sem_fwd_r.at[ch, which, j, k - 1],
            device_id=(c_me, to), device_id_type=MESH,
        )

    def relay(which, j, back_by):
        step = 1 if back_by == 0 else -1
        if which == 0:
            ref = place_of(ring(y, -step, other), ring(z, -j, side), 0, 0)
            to = ring(y, step, other) * side + z
        else:
            ref = place_of(ring(y, -j, other), ring(z, -step, side), 1, 0)
            to = y * side + ring(z, step, side)
        ref = ref.at[pl.ds(back_by * quarter, quarter)]
        return pltpu.make_async_remote_copy(
            ref, ref, sem_rel.at[which, j, back_by, 0], sem_rel.at[which, j, back_by, 1],
            device_id=(c_me, to), device_id_type=MESH,
        )

    for ch in range(2):
        for k in (1, 3, 2):
            near(ch, 0, k).start()
            near(ch, 1, k).start()
        for k in (1, 3) if ch == 0 else (1, 3, 2):
            forward(ch, 0, 0, k).start()
            forward(ch, 1, 0, k).start()
    gather_own = [
        pltpu.make_async_copy(ja, ga.at[pl.ds(pl.multiple_of(d_me * tok, tok), tok)], sem_own.at[0]),
        pltpu.make_async_copy(jb, gb.at[d_me], sem_own.at[1]),
    ]
    hidden_own.wait()
    for c in gather_own:
        c.start()
    each(2, lambda i: late_queries(i + 2))
    send_out(last, 1)
    for j in (1, 3, 2):
        for which in range(2):
            near(0, which, j).wait_recv()
            for k in (1, 3):
                forward(0, which, j, k).start()
    for j in (0, 1, 3, 2):
        for which in range(2):
            for k in (1, 3):
                forward(0, which, j, k).wait_recv()
                relay(which, j, k // 2).start()
    for j in (1, 3, 2):
        for which in range(2):
            near(1, which, j).wait_recv()
            for k in (1, 3, 2):
                forward(1, which, j, k).start()
    each(ndp - 1, lambda i: hidden_copy(i).wait())
    for c in gather_own:
        c.wait()
    for j in (0, 1, 3, 2):
        for which in range(2):
            for back_by in range(2):
                relay(which, j, back_by).wait_recv()

    def part_copy(ch, i):
        to = cp_dev(i + 1)
        src, dst = ((pa, ra), (pb, rb))[ch]
        return pltpu.make_async_remote_copy(
            src.at[to], dst.at[i], sem_ps.at[ch, i], sem_pr.at[ch, i],
            device_id=(to, d_me), device_id_type=MESH,
        )

    block = 4 * PIECE

    def product(c):
        d = dot(hr[pl.ds(pl.multiple_of(c * block, block), block), :], ga[...], 1, 0).astype(BF)
        for i in range(4):
            pa[c * 4 + i] = d[i * PIECE : (i + 1) * PIECE]

    each(ncp // 4, product)
    each(ncp - 1, lambda i: part_copy(0, i).start())
    for j in range(4):
        for which in range(2):
            for k in (1, 2, 3):
                forward(1, which, j, k).wait_recv()

    def unfold(i):
        for w in range(2):
            at = i * tok + w * half
            gc[pl.ds(pl.multiple_of(at, half), half), :128] = gb[i, w, :half, :]
            folded = gb[i, w, half:, :].astype(F32)
            gc[pl.ds(pl.multiple_of(at, quarter), quarter), 128:] = folded.astype(BF)
            gc[pl.ds(pl.multiple_of(at + quarter, quarter), quarter), 128:] = pltpu.roll(folded, ROPE, 1).astype(BF)

    each(ndp, unfold)

    def product_rest(c):
        d = dot(hr[pl.ds(pl.multiple_of(c * block, block), block), :], gc[...], 1, 0)
        for i in range(4):
            piece = d[i * PIECE : (i + 1) * PIECE]
            pb[c * 4 + i, :PIECE, :] = piece[:, :128].astype(BF)
            folded = jnp.where(low[: PIECE // 2], piece[: PIECE // 2, 128:], pltpu.roll(piece[PIECE // 2 :, 128:], ROPE, 1))
            pb[c * 4 + i, PIECE:, :] = folded.astype(BF)

    each(ncp // 4, product_rest)
    each(ncp - 1, lambda i: part_copy(1, i).start())
    for c in halo + back_copies:
        c.wait_send()
    for which in range(2):
        for ch in range(2):
            for k in (1, 2, 3):
                near(ch, which, k).wait_send()
            for j in range(4):
                for k in (1, 3) if ch == 0 else (1, 2, 3):
                    forward(ch, which, j, k).wait_send()
        for j in range(4):
            for back_by in range(2):
                relay(which, j, back_by).wait_send()
    first = pa[c_me].astype(F32)
    for i in range(ncp - 1):
        part_copy(0, i).wait_recv()
        first = first + ra[i].astype(F32)
    dw[:, :FIRST] = first[:rows_dev]
    rest = pb[c_me].astype(F32)
    for i in range(ncp - 1):
        part_copy(1, i).wait_recv()
        rest = rest + rb[i].astype(F32)
    dw[:, FIRST:lat] = rest[:rows_dev]
    dw[: PIECE // 2, lat:] = rest[PIECE:, :ROPE]
    dw[PIECE // 2 :, lat:] = pltpu.roll(rest[PIECE:], ROPE, 1)[: rows_dev - PIECE // 2, :ROPE]

    for ch in range(2):
        each(ncp - 1, lambda i: part_copy(ch, i).wait_send())

    def finish(n):
        layer, half = n // 2, lax.rem(n, 2)
        for c in out_own(layer, half):
            c.wait()

        def one(i):
            for c in out_copies(layer, half, i):
                c.wait()

        each(ncp - 1, one)

    each(2 * layers, finish)


def pass_on(*refs):
    count = (len(refs) - 2) // 3
    came, went = refs[-2:]
    moves = []
    for i in range(count):
        src, dst, held = refs[i], refs[count + i], refs[2 * count + i]
        pieces = [(0, slice(None))]
        if len(src.shape) > 2:
            cut = src.shape[1] // 4
            pieces = [(n, (n // 4, slice(n % 4 * cut, (n % 4 + 1) * cut))) for n in range(4 * src.shape[0])]
        for n, at in pieces:
            moves.append(
                (
                    pltpu.make_async_copy(src.at[at], held.at[at], came.at[i, n]),
                    pltpu.make_async_copy(held.at[at], dst.at[at], went.at[i, n]),
                )
            )
    for load, _ in moves:
        load.start()
    for load, store in moves:
        load.wait()
        store.start()
    for _, store in moves:
        store.wait()


def on_device(q_nope, q_rope, grad_out, latent, key_rope, hidden_in, w_uk, w_uv, doc_lengths, plan):
    ncp = lax.axis_size("cp")
    ndp = lax.axis_size("dp")
    side = math.isqrt(ndp)
    layers, _, tok, heads, head = q_nope.shape
    wide = q_rope.shape[3]
    lat = latent.shape[2]
    model = hidden_in.shape[2]
    ext = lat + 2 * ROPE
    rows = tok * heads
    smem = pl.BlockSpec(memory_space=pltpu.SMEM)
    hbm = pl.BlockSpec(memory_space=pl.ANY)
    vmem = pl.BlockSpec(memory_space=pltpu.VMEM)
    dma = pltpu.SemaphoreType.DMA
    results = pl.pallas_call(
        functools.partial(kernel, ncp, ndp, side),
        out_shape=(
            jax.ShapeDtypeStruct((layers, tok, heads, head), BF),
            jax.ShapeDtypeStruct((layers, tok, wide), BF),
            jax.ShapeDtypeStruct((tok, lat), BF),
            jax.ShapeDtypeStruct((ROPE, tok), BF),
            jax.ShapeDtypeStruct((model // (ncp * ndp), lat + ROPE), F32),
        ),
        in_specs=[smem, smem] + [hbm] * 8,
        out_specs=(hbm, hbm, vmem, vmem, vmem),
        scratch_shapes=[
            pltpu.VMEM((layers, rows, head), BF),
            pltpu.VMEM((layers, tok, wide), BF),
            pltpu.VMEM((layers, rows, head), BF),
            pltpu.VMEM((MARGIN + tok, ext), BF),
            pltpu.VMEM((ROPE, tok), BF),
            pltpu.VMEM((tok, model), BF),
            pltpu.VMEM(w_uk.shape, BF),
            pltpu.VMEM(w_uv.shape, BF),
            pltpu.VMEM((layers, tok * PITCH + 40, head), F32),
            pltpu.VMEM((layers, tok * PITCH + 40, head), F32),
            pltpu.VMEM((ncp, tok // ncp * OUT_PITCH + 24, head), F32),
            pltpu.VMEM((ncp, tok // ncp, wide // 2), BF),
            pltpu.VMEM((2, 2, HG * SUB, ext), BF),
            pltpu.VMEM((2, 2, HG * SUB, lat), BF),
            pltpu.VMEM((HG, tok, lat), BF),
            pltpu.VMEM((heads // HG, 2, HG * SUB, WIN), BF),
            pltpu.VMEM((2, SUB, WIN), F32),
            pltpu.VMEM((MARGIN + tok, ext), F32),
            pltpu.VMEM((ncp, layers, 2, tok // ncp, heads // 2, head), BF),
            pltpu.VMEM((ncp, layers, 2, tok // ncp, wide // 2), BF),
            pltpu.VMEM((model // ncp, tok), F32),
            pltpu.VMEM((ndp, ncp * PIECE, tok), BF),
            pltpu.VMEM((ncp * PIECE, ndp * tok), BF),
            pltpu.VMEM((MARGIN, ext), BF),
            pltpu.VMEM((tok, ext), BF),
            pltpu.VMEM((MARGIN - tok, ext), BF),
            pltpu.VMEM((tok, FIRST), BF),
            pltpu.VMEM((2, tok // 2 + tok // 4, 128), BF),
            pltpu.VMEM((ndp * tok, FIRST), BF),
            pltpu.VMEM((ndp, 2, tok // 2 + tok // 4, 128), BF),
            pltpu.VMEM((ndp * tok, 256), BF),
            pltpu.VMEM((ncp, PIECE, FIRST), BF),
            pltpu.VMEM((ncp, PIECE + PIECE // 2, 128), BF),
            pltpu.VMEM((ncp - 1, PIECE, FIRST), BF),
            pltpu.VMEM((ncp - 1, PIECE + PIECE // 2, 128), BF),
            dma((layers, 3)),
            dma((layers, heads // HG, 2)),
            dma((3,)),
            dma((4,)),
            dma((ndp - 1,)),
            dma((ndp - 1,)),
            dma((layers, 2, ncp - 1, 2)),
            dma((layers, 2, ncp - 1, 2)),
            dma((layers, 2, 2)),
            dma((4,)),
            dma((2, 2, 2, 3)),
            dma((2, 2, 4, 3)),
            dma((2, 2, 4, 3)),
            dma((2, 4, 2, 2)),
            dma((2, ncp - 1)),
            dma((2, ncp - 1)),
            dma((2,)),
        ],
        compiler_params=pltpu.CompilerParams(
            collective_id=0, has_side_effects=True, vmem_limit_bytes=60 * 1024 * 1024
        ),
        name="attention_backward",
    )(
        doc_lengths,
        plan,
        q_nope.reshape(layers, rows, head),
        q_rope[:, 0],
        grad_out.reshape(layers, rows, head),
        latent[0],
        key_rope[0],
        hidden_in[0],
        w_uk,
        w_uv,
    )
    dqn, dqr, dlat, dkr, dw = pl.pallas_call(
        pass_on,
        out_shape=tuple(jax.ShapeDtypeStruct(r.shape, r.dtype) for r in results),
        in_specs=[hbm] * 5,
        out_specs=(hbm,) * 5,
        scratch_shapes=[pltpu.VMEM(r.shape, r.dtype) for r in results] + [dma((5, 8)), dma((5, 8))],
        name="pass_on",
    )(*results)
    return (
        dqn.reshape(q_nope.shape),
        dqr.reshape(q_rope.shape),
        dlat[None],
        dkr[None],
        dw,
    )


def solution(mesh):
    placed = (
        P(None, "dp", "cp", None, None),
        P(None, "dp", "cp", None),
        P(None, "dp", "cp", None, None),
        P("dp", "cp", None),
        P("dp", None, "cp"),
        P("dp", "cp", None),
        P(),
        P(),
        P("dp", None),
        P("dp", None, None),
    )
    return jax.shard_map(
        on_device,
        mesh=mesh,
        in_specs=placed,
        out_specs=(
            P(None, "dp", "cp", None, None),
            P(None, "dp", "cp", None),
            P("dp", "cp", None),
            P("dp", None, "cp"),
            P(("cp", "dp"), None),
        ),
        check_vma=False,
    )
```
